512 devices in a mesh: section: 2 (over y_hi), dp: 64 (over y_lo, z, core), tp: 4 (over x).
Axes of the slice: x: 4, y: 8 (y_hi: 2, y_lo: 4; y = y_hi * 4 + y_lo), z: 8, core: 2. Of those that a mesh axis runs over, the one named last changes fastest.
Arguments:
- cache: bfloat16 [128, 96, 64, 576], P(('section', 'dp'), 'tp'), may hold values from -6 to 6
- sent: bfloat16 [128, 16, 64, 576], P(('section', 'dp'), 'tp'), may hold values from -6 to 6
- slot_of: int32 [128, 16], P(('section', 'dp'), 'tp'), may hold values from 0 to 23, as said below
- table: int32 [128, 96], P(('section', 'dp'), 'tp'), may hold values from 0 to 95, each once within a row
- lengths: int32 [128], P(('section', 'dp')), may hold values from 64 to 6144
- new_kv: bfloat16 [128, 2, 576], P(('section', 'dp')), may hold values from -6 to 6
- queries: bfloat16 [128, 2, 64, 576], P(('section', 'dp')), may hold values from -24 to 24
- resid: bfloat16 [128, 2, 7168], P(('section', 'dp'), None, 'tp'), may hold values from -6 to 6
- gain: float32 [7168], P('tp'), may hold values from 0.25 to 1.75
- w_ov: bfloat16 [32768, 7168], P(('section', 'dp'), 'tp'), may hold values from -0.25 to 0.25
- w_gate: bfloat16 [7168, 18432], P('tp', ('section', 'dp')), may hold values from -0.0625 to 0.0625
- w_up: bfloat16 [7168, 18432], P('tp', ('section', 'dp')), may hold values from -0.0625 to 0.0625
- w_down: bfloat16 [18432, 7168], P(('section', 'dp'), 'tp'), may hold values from -0.046875 to 0.046875
Outputs:
- output: bfloat16 [128, 2, 7168], P(('section', 'dp'), None, 'tp')
The draws below stay inside these ranges and needn't reach their ends.
Inputs may be any that keep to these rules, and one draw needn't show every extreme that they name: `slot_of`: within each row, the 4 entries that belong to one device of tp name different slots.
All inputs are finite; a program needn't handle non-finite values.
Results may differ from the reference program's by a relative error of at most 0.011.
Values may be sent and summed in bfloat16 or wider, within the bound.
A program may use at most 128 MiB of HBM per device.

```python
import jax
import jax.numpy as jnp
from jax import lax

D = 7168
FF = 18432
LAT = 512
H = 64
PAGE = 64
SLOTS = 24
SEND = 4
KVW = 576
ROWS = 128
N_SECTION = 2
N_TP = 4


def shared_newest(key):
    values = jax.random.normal(jax.random.fold_in(key, 101), (ROWS, 2, KVW), jnp.float32)
    return jnp.clip(values, -6.0, 6.0)


def draw_new_kv(key, part):
    newest = shared_newest(key)
    return newest.astype(jnp.bfloat16)


def draw_queries(key, part):
    newest = shared_newest(key)
    first = newest[:, 0, :].astype(jnp.bfloat16).astype(jnp.float32)
    length_sq = jnp.sum(first * first, axis=-1)
    direction = first / (length_sq[:, None] * 192.0 ** (-0.5))
    key = jax.random.fold_in(key, 7)
    values = jax.random.normal(key, (ROWS, 2, H, KVW), jnp.float32)
    target_base = jnp.where(jnp.arange(H) == 0, 110.0, 230.0)
    jitter = jax.random.uniform(jax.random.fold_in(key, 11), (ROWS, 1, H), jnp.float32, 0.0, 40.0)
    target = target_base[None, None, :] + jitter
    aligned = target[..., None] * direction[:, None, None, :]
    head_mask = jnp.arange(H) < 2
    values = jnp.where(head_mask[None, None, :, None], aligned, values)
    return jnp.clip(values, -24.0, 24.0).astype(jnp.bfloat16)


def draw_slot_of(key, part):
    key = jax.random.fold_in(key, 5)
    row_keys = jax.random.split(key, ROWS * N_TP)
    chosen = jax.vmap(lambda row_key: jax.random.permutation(row_key, SLOTS)[:SEND])(row_keys)
    return chosen.reshape(ROWS, N_TP * SEND).astype(jnp.int32)


def set_ends(entries, stream_key, least, largest):
    place = [jax.random.randint(jax.random.fold_in(stream_key, axis), (), 0, length) for axis, length in enumerate(entries.shape)]
    widest = entries.shape.index(max(entries.shape))
    next_to = place[:widest] + [(place[widest] + 1) % entries.shape[widest]] + place[widest + 1:]
    return entries.at[tuple(place)].set(least).at[tuple(next_to)].set(largest)


def steps_of(own_key, extent, pieces, smallest, top_value):
    def one(dim, parts):
        heights = jax.random.uniform(jax.random.fold_in(jax.random.fold_in(own_key, 6), dim), (parts,), jnp.float32, smallest / len(pieces), top_value / len(pieces))
        return jnp.repeat(jnp.exp(heights), extent[dim] // parts).reshape((-1,) + (1,) * (len(extent) - dim - 1))

    factor_of = one(*pieces[0])
    for cut in pieces[1:]:
        factor_of = factor_of * one(*cut)
    return factor_of


def noise(key, dims, spread, bound, cuts=(), held_as=jnp.bfloat16):
    level = steps_of(key, dims, cuts, -0.22, 0.18) if cuts else 1.0
    result = jax.random.normal(key, dims, jnp.float32) * spread * level
    return jnp.minimum(jnp.maximum(result, -bound), bound).astype(held_as)


def setup_inputs(seed: int = 0) -> dict:
    arg_keys = jax.random.split(jax.random.key(seed), 14)
    return {
        "cache": noise(arg_keys[0], (ROWS, N_TP * SLOTS, PAGE, KVW), 1.0, 6.0, ((0, 128), (1, 4))),
        "sent": noise(arg_keys[1], (ROWS, N_TP * SEND, PAGE, KVW), 1.0, 6.0, ((0, 128), (1, 4))),
        "slot_of": draw_slot_of(jax.random.fold_in(arg_keys[13], 71), 0),
        "table": jax.vmap(lambda own: jax.random.permutation(own, N_TP * SLOTS))(jax.random.split(arg_keys[3], ROWS)).reshape((ROWS, N_TP * SLOTS)).astype(jnp.int32),
        "lengths": set_ends(jax.random.randint(arg_keys[4], (ROWS,), PAGE, N_TP * SLOTS * PAGE + 1), jax.random.fold_in(arg_keys[4], 1), PAGE, N_TP * SLOTS * PAGE).astype(jnp.int32),
        "new_kv": draw_new_kv(jax.random.fold_in(arg_keys[13], 71), 0),
        "queries": draw_queries(jax.random.fold_in(arg_keys[13], 71), 0),
        "resid": noise(arg_keys[7], (ROWS, 2, D), 1.0, 6.0, ((0, 128), (2, 4))),
        "gain": jnp.clip(1.0 + 0.15 * jax.random.normal(arg_keys[8], (D,), jnp.float32), 0.25, 1.75),
        "w_ov": noise(arg_keys[9], (H * LAT, D), LAT ** -0.5, 0.25, ((0, 128), (1, 4))),
        "w_gate": noise(arg_keys[10], (D, FF), D ** -0.5, 0.0625, ((0, 4), (1, 128))),
        "w_up": noise(arg_keys[11], (D, FF), D ** -0.5, 0.0625, ((0, 4), (1, 128))),
        "w_down": noise(arg_keys[12], (FF, D), FF ** -0.5, 0.046875, ((0, 128), (1, 4))),
    }


SCALE = 192.0 ** (-0.5)
EPS = 1e-06

def row_attention(key_rows, usable, query_row, newest):
    query_wide = query_row.astype(jnp.float32)
    key_wide = key_rows.astype(jnp.float32)
    newest_wide = newest.astype(jnp.float32)
    scores = jnp.einsum('phk,nk->phn', query_wide, key_wide) * SCALE
    scores = jnp.where(usable[None, None, :], scores, -jnp.inf)
    extra = jnp.einsum('phk,ek->phe', query_wide, newest_wide) * SCALE
    causal = jnp.arange(2, dtype=jnp.int32)[:, None] >= jnp.arange(2, dtype=jnp.int32)[None, :]
    extra = jnp.where(causal[:, None, :], extra, -jnp.inf)
    top_score = jnp.maximum(lax.optimization_barrier(jnp.max(scores, axis=-1)), lax.optimization_barrier(jnp.max(extra, axis=-1)))
    weights = jnp.exp(scores - top_score[..., None])
    extra_weights = jnp.exp(extra - top_score[..., None])
    prob_sum = lax.optimization_barrier(jnp.sum(weights, axis=-1)) + lax.optimization_barrier(jnp.sum(extra_weights, axis=-1))
    rounded = lax.optimization_barrier(weights.astype(jnp.bfloat16)).astype(jnp.float32)
    extra_rounded = lax.optimization_barrier(extra_weights.astype(jnp.bfloat16)).astype(jnp.float32)
    weighted = jnp.einsum('phn,nl->phl', rounded, key_wide[:, :LAT])
    weighted = weighted + jnp.einsum('phe,el->phl', extra_rounded, newest_wide[:, :LAT])
    return (weighted / prob_sum[..., None]).astype(jnp.bfloat16)

def reference(cache, sent, slot_of, table, lengths, new_kv, queries, resid, gain, w_ov, w_gate, w_up, w_down):
    halves = sent.reshape((N_SECTION, ROWS // N_SECTION) + sent.shape[1:])
    received = jnp.flip(halves, 0).reshape(sent.shape)
    tp_block = jnp.arange(N_TP * SEND, dtype=jnp.int32) // SEND
    where_to = (tp_block[None, :] * SLOTS + slot_of).astype(jnp.int32)

    def one_row(inputs):
        page_rows, targets, incoming, page_order, length, query_row, newest = inputs
        filled = page_rows.at[targets].set(incoming)
        position = page_order[:, None] * PAGE + jnp.arange(PAGE, dtype=jnp.int32)[None, :]
        usable = (position < length).reshape(-1)
        return row_attention(filled.reshape(-1, KVW), usable, query_row, newest)
    latent = lax.map(one_row, (cache, where_to, received, table, lengths, queries, new_kv))
    flat = latent.reshape(ROWS * 2, H * LAT)
    attended = jnp.dot(flat, w_ov, preferred_element_type=jnp.float32).reshape(ROWS, 2, D)
    resid_sum = resid.astype(jnp.float32) + attended
    mean_square = lax.optimization_barrier(jnp.mean(resid_sum * resid_sum, axis=-1)).reshape(ROWS * 2, 1)
    normed = (resid_sum * gain).astype(jnp.bfloat16).reshape(ROWS * 2, D)
    factor = lax.rsqrt(mean_square + EPS)
    gate_sum = jnp.dot(normed, w_gate, preferred_element_type=jnp.float32) * factor
    up_sum = jnp.dot(normed, w_up, preferred_element_type=jnp.float32) * factor
    hidden = (jax.nn.silu(gate_sum) * up_sum).astype(jnp.bfloat16)
    down = jnp.dot(hidden, w_down, preferred_element_type=jnp.float32).reshape(ROWS, 2, D)
    return (resid_sum + down).astype(jnp.bfloat16)
```

```python
import functools

import jax
import jax.numpy as jnp
from jax import lax
from jax.experimental import pallas as pl
from jax.experimental.pallas import tpu as pltpu
from jax.sharding import PartitionSpec as P

D = 7168
LAT = 512
SCALE = 192.0 ** (-0.5)
EPS = 1e-06
LOW = -1e30
FLOOR = -1e20
MESH = pl.DeviceIdType.MESH
BF = jnp.bfloat16
F32 = jnp.float32
HALF = 896
PAIRS = 7

NT = (((1,), (1,)), ((), ()))


def dot(a, b):
    return jnp.dot(a, b, preferred_element_type=F32)


def swap_rows(x, scratch):
    blocks = x.shape[1] // 128
    for c in range(2):
        for a in range(8):
            for p in range(2):
                row = c * 128 + a * 16 + p * 8
                for n in range(blocks):
                    scratch[n, pl.ds(c * 128 + p * 8 + a, 8, stride=16), :] = x[
                        row : row + 8, n * 128 : (n + 1) * 128
                    ]
    return jnp.concatenate([scratch[n] for n in range(blocks)], axis=1)


def kernel(
    lengths_ref,
    table_ref,
    slot_ref,
    new_ref,
    resid_ref,
    gain_ref,
    cache_ref,
    sent_ref,
    query_ref,
    wov_ref,
    wgate_ref,
    wup_ref,
    wdown_ref,
    out_ref,
    kv,
    kx,
    kn,
    qs,
    wov,
    wg,
    wu,
    wc,
    wd,
    xs_send,
    xs_recv,
    lat,
    l1,
    tf,
    tb,
    a1,
    a2,
    perm,
    core_send,
    core_recv,
    tot,
    send1,
    recv1,
    pack,
    send2,
    recv2,
    rsd,
    gpk,
    recv3,
    unp,
    n0,
    n1,
    gs,
    recvx,
    hid,
    flat,
    load_sem,
    hand_sem,
    xs_ss,
    xs_rs,
    ly_ss,
    ly_rs,
    lx_ss,
    lx_rs,
    lz_ss,
    lz_rs,
    core_ss,
    core_rs,
    p1_ss,
    p1_rs,
    p2_ss,
    p2_rs,
    p3_ss,
    p3_rs,
    p4_ss,
    p4_rs,
    p5_ss,
    p5_rs,
    gx_ss,
    gx_rs,
    hx_ss,
    hx_rs,
):
    dp = lax.axis_index("dp")
    t = lax.axis_index("tp")
    Y = lax.axis_index("section") * 4 + dp // 16
    zc = dp % 16
    z = zc // 2
    c = zc % 2
    sib = 1 - c

    def dev(y_, zc_, t_):
        return (y_ // 4, (y_ % 4) * 16 + zc_, t_)

    def along(s, first, k):
        if (s == 0) == first:
            return dev(Y, ((z + k) % 8) * 2 + c, t)
        return dev((Y + k) % 8, zc, t)

    here = (z, Y)
    there = (Y, z)
    sibling = dev(Y, z * 2 + sib, t)

    def remote(src, dst, ss, rs, to):
        return pltpu.make_async_remote_copy(
            src_ref=src, dst_ref=dst, send_sem=ss, recv_sem=rs, device_id=to, device_id_type=MESH
        )

    def landed(region, ss, rs):
        remote(region, region, ss, rs, sibling).wait_recv()

    loads = [
        pltpu.make_async_copy(cache_ref.at[0], kv, load_sem.at[0]),
        pltpu.make_async_copy(query_ref.at[0], qs, load_sem.at[1]),
        pltpu.make_async_copy(wov_ref, wov, load_sem.at[2]),
        pltpu.make_async_copy(wgate_ref, wg, load_sem.at[3]),
        pltpu.make_async_copy(wup_ref, wu, load_sem.at[4]),
        pltpu.make_async_copy(wdown_ref, wd.at[pl.ds(0, 144)], load_sem.at[5]),
    ]
    for load in loads:
        load.start()

    barrier = pltpu.get_barrier_semaphore()
    for k in range(1, 8):
        pl.semaphore_signal(barrier, inc=1, device_id=dev((Y + k) % 8, zc, t), device_id_type=MESH)
    for k in range(1, 16):
        pl.semaphore_signal(barrier, inc=1, device_id=dev(Y, (zc + k) % 16, t), device_id_type=MESH)
    for k in range(1, 4):
        pl.semaphore_signal(barrier, inc=1, device_id=dev(Y, zc, (t + k) % 4), device_id_type=MESH)
    pl.semaphore_wait(barrier, 25)

    hand = remote(sent_ref.at[0], kx, hand_sem.at[0], hand_sem.at[1], dev((Y + 4) % 8, zc, t))
    hand.start()

    resid = resid_ref[0].astype(F32)
    for s in range(2):
        rsd[s] = jnp.zeros((16, 128), F32)
        gpk[s] = jnp.zeros((16, 128), F32)
        for p in range(2):
            for k in range(PAIRS):
                n = s * PAIRS + k
                rsd[s, p * 8 + k : p * 8 + k + 1, :] = resid[p : p + 1, n * 128 : (n + 1) * 128]
                gpk[s, p * 8 + k : p * 8 + k + 1, :] = gain_ref[0:1, n * 128 : (n + 1) * 128]
    wd[pl.ds(144, 112)] = jnp.zeros((112, 1792), BF)
    kn[...] = jnp.zeros((128, 576), BF)
    kn[0:2, :] = new_ref[0]

    loads[3].wait()
    loads[4].wait()
    for r in range(0, 1792, 256):
        rows = pl.ds(r, 256)
        gate_w = wg[rows]
        up_w = wu[rows]
        wc[rows, 0:128] = gate_w[:, 0:128]
        wc[rows, 128:256] = up_w[:, 0:128]
        wc[rows, 256:384] = jnp.concatenate(
            [
                gate_w[:, 128:144].astype(F32),
                up_w[:, 128:144].astype(F32),
                jnp.zeros((256, 96), F32),
            ],
            axis=1,
        ).astype(BF)

    lane = lax.broadcasted_iota(jnp.int32, (1, 128), 1)
    inside = lane % 64
    length = lengths_ref[0]

    def bias_of(first, second):
        return jnp.where(inside < jnp.where(lane < 64, first, second), 0.0, LOW)

    limits = []
    for slot in range(24):
        limit = length - table_ref[0, slot] * 64
        for e in range(4):
            limit = jnp.where(slot_ref[0, e] == slot, 0, limit)
        limits.append(limit)
    bias = jnp.concatenate([bias_of(limits[i], limits[i + 1]) for i in range(0, 24, 2)], axis=1)
    late = [length - table_ref[0, slot_ref[0, e]] * 64 for e in range(4)]
    bias_x = jnp.concatenate([bias_of(late[0], late[1]), bias_of(late[2], late[3])], axis=1)
    head = lax.broadcasted_iota(jnp.int32, (128, 128), 0)
    entry = lax.broadcasted_iota(jnp.int32, (128, 128), 1)
    fresh = jnp.where(t == 0, 1, 0)
    bias_n = jnp.where(entry < jnp.where(head < 64, 1, 2) * fresh, 0.0, LOW)

    loads[0].wait()
    loads[1].wait()
    q = qs[...].reshape(128, 576)
    keys = kv[...].reshape(1536, 576)
    scores = lax.dot_general(q, keys, NT, preferred_element_type=F32) * SCALE + bias
    scores_n = lax.dot_general(q, kn[...], NT, preferred_element_type=F32) * SCALE + bias_n
    top = jnp.maximum(
        jnp.max(scores, axis=1, keepdims=True), jnp.max(scores_n, axis=1, keepdims=True)
    )
    top = jnp.maximum(top, FLOOR)
    w = jnp.exp(scores - top)
    w_n = jnp.exp(scores_n - top)
    total = jnp.sum(w, axis=1, keepdims=True) + jnp.sum(w_n, axis=1, keepdims=True)
    acc = dot(w.astype(BF), keys[:, :LAT]) + dot(w_n.astype(BF), kn[:, :LAT])

    hand.wait_recv()
    keys = kx[...].reshape(256, 576)
    scores = lax.dot_general(q, keys, NT, preferred_element_type=F32) * SCALE + bias_x
    top_all = jnp.maximum(top, jnp.max(scores, axis=1, keepdims=True))
    w = jnp.exp(scores - top_all)
    shrink = jnp.exp(top - top_all)
    total = total * shrink + jnp.sum(w, axis=1, keepdims=True)
    acc = acc * shrink + dot(w.astype(BF), keys[:, :LAT])
    total = jnp.where(total > 0.0, total, 1.0)
    acc = acc / total
    lse = top_all + jnp.log(total)
    hi = lse.astype(BF).astype(F32)
    mid = (lse - hi).astype(BF).astype(F32)
    low = lse - hi - mid
    tail = jnp.where(entry < 32, hi, jnp.where(entry < 64, mid, low))
    for n in range(4):
        flat[n] = acc[:, n * 128 : (n + 1) * 128]
    flat[4] = tail

    def part_of(dest, j):
        block = (Y + dest + 4 * j) % 8
        rows = []
        for p in range(2):
            at = pl.ds(pl.multiple_of(p * 64 + block * 8, 8), 8)
            rows.append(jnp.concatenate([flat[n, at, :] for n in range(5)], axis=1))
        return jnp.concatenate(rows, axis=0)

    xs = []
    for k in range(1, 4):
        to = (t + k) % 4
        for j in range(2):
            xs_send[k, j] = part_of(to, j).astype(BF)
        copy = remote(xs_send.at[k], xs_recv.at[k], xs_ss.at[k], xs_rs.at[k], dev(Y, zc, to))
        copy.start()
        xs.append(copy)
    mine = [part_of(t, j) for j in range(2)]
    for copy in xs:
        copy.wait_recv()
    for j in range(2):
        parts = [mine[j]] + [xs_recv[k, j].astype(F32) for k in range(1, 4)]
        lses = [part[:, 512:513] + part[:, 544:545] + part[:, 576:577] for part in parts]
        best = functools.reduce(jnp.maximum, lses)
        shares = [jnp.exp(value - best) for value in lses]
        norm = functools.reduce(jnp.add, shares)
        mixed = functools.reduce(
            jnp.add, [part[:, :LAT] * share for part, share in zip(parts, shares)]
        )
        lat[j] = (mixed / norm).astype(BF)

    ly = [
        remote(
            lat.at[j], l1.at[t * 2 + j], ly_ss.at[j], ly_rs.at[j], dev((Y + t + 4 * j) % 8, zc, t)
        )
        for j in range(2)
    ]
    ly[1].start()

    @pl.when(t != 0)
    def _():
        ly[0].start()

    @pl.when(t == 0)
    def _():
        l1[0] = lat[0]

    for copy in xs:
        copy.wait_send()

    @pl.when(t != 0)
    def _():
        ly[0].wait_recv()

    ly[1].wait_recv()
    lx = []
    own = l1.at[pl.ds(t * 2, 2)]
    for k in range(1, 4):
        copy = remote(own, own, lx_ss.at[k], lx_rs.at[k], dev(Y, zc, (t + k) % 4))
        copy.start()
        lx.append(copy)
    ly[1].wait_send()

    @pl.when(t != 0)
    def _():
        ly[0].wait_send()

    for k in range(4):
        source = (t - k + 4) % 4
        if k:
            landed(l1.at[pl.ds(source * 2, 2)], lx_ss.at[k], lx_rs.at[k])
        for j in range(2):
            block = l1[source * 2 + j].astype(F32)
            y_from = (Y - source - 4 * j + 8) % 8
            for p in range(2):
                for n in range(4):
                    tf[n, pl.ds(p * 8 + y_from, 8, stride=16), :] = block[
                        p * 8 : p * 8 + 8, n * 128 : (n + 1) * 128
                    ]
    for n in range(2):
        tb[n] = jnp.concatenate([tf[2 * n], tf[2 * n + 1]], axis=1).astype(BF)
    lz = []

    def a_rows(zc_):
        return pl.ds(pl.multiple_of(((zc_ % 2) * 8 + zc_ // 2) * 16, 16), 16)

    for k in range(1, 16):
        to = (zc + k) % 16
        copy = remote(
            tb.at[to % 2, pl.ds(pl.multiple_of((to // 2) * 16, 16), 16)],
            a1.at[a_rows(zc)],
            lz_ss.at[k],
            lz_rs.at[k],
            dev(Y, to, t),
        )
        copy.start()
        lz.append(copy)
    a1[a_rows(zc), :] = tb[c, pl.ds(pl.multiple_of(z * 16, 16), 16), :]
    for copy in lx:
        copy.wait_send()
    loads[2].wait()
    loads[5].wait()
    for k in range(1, 16):
        landed(a1.at[a_rows((zc - k + 16) % 16)], lz_ss.at[k], lz_rs.at[k])
    wide = a1[...].astype(F32)
    a2[...] = swap_rows(wide, perm).astype(BF)
    for copy in lz:
        copy.wait_send()

    def reduced(u, operands, weight):
        started = []
        ours = []
        for s in range(2):
            columns = slice(s * HALF, (s + 1) * HALF)
            rows = pl.ds(pl.multiple_of(sib * 128, 128), 128)
            core_send[u, s] = dot(operands[s][rows, :], weight[:, columns]).astype(BF)
            copy = remote(
                core_send.at[u, s],
                core_recv.at[u, s],
                core_ss.at[u, s],
                core_rs.at[u, s],
                sibling,
            )
            copy.start()
            started.append(copy)
        for s in range(2):
            columns = slice(s * HALF, (s + 1) * HALF)
            rows = pl.ds(pl.multiple_of(c * 128, 128), 128)
            tot[s] = dot(operands[s][rows, :], weight[:, columns])
        first = []
        for s in range(2):
            started[s].wait_recv()
            tot[s] = tot[s] + core_recv[u, s].astype(F32)
            send1[u, s] = tot[s].astype(BF)
            copies = []
            for k in range(1, 8):
                block = (here[s] + k) % 8
                copy = remote(
                    send1.at[u, s, pl.ds(pl.multiple_of(block * 16, 16), 16)],
                    recv1.at[u, s, k],
                    p1_ss.at[u, s, k],
                    p1_rs.at[u, s, k],
                    along(s, True, k),
                )
                copy.start()
                copies.append(copy)
            first.append(copies)
        for copy in started:
            copy.wait_send()
        second = []
        for s in range(2):
            part = tot[s, pl.ds(pl.multiple_of(here[s] * 16, 16), 16), :]
            for k in range(1, 8):
                first[s][k - 1].wait_recv()
                part = part + recv1[u, s, k].astype(F32)
            for p in range(2):
                for k in range(PAIRS):
                    pack[s, pl.ds(p * 8 + k, 8, stride=16), :] = part[
                        p * 8 : p * 8 + 8, k * 128 : (k + 1) * 128
                    ]
                pack[s, pl.ds(p * 8 + PAIRS, 8, stride=16), :] = jnp.zeros((8, 128), F32)
            send2[u, s] = pack[s].astype(BF)
            copies = []
            for k in range(1, 8):
                block = (there[s] + k) % 8
                copy = remote(
                    send2.at[u, s, pl.ds(pl.multiple_of(block * 16, 16), 16)],
                    recv2.at[u, s, k],
                    p2_ss.at[u, s, k],
                    p2_rs.at[u, s, k],
                    along(s, False, k),
                )
                copy.start()
                copies.append(copy)
            second.append(copies)
        for copies in first:
            for copy in copies:
                copy.wait_send()
        result = []
        for s in range(2):
            part = pack[s, pl.ds(pl.multiple_of(there[s] * 16, 16), 16), :]
            for k in range(1, 8):
                second[s][k - 1].wait_recv()
                part = part + recv2[u, s, k].astype(F32)
            result.append(part)
        return result, [copy for copies in second for copy in copies]

    attended, pending = reduced(0, (a1, a2), wov)

    sums = []
    squares = []
    for s in range(2):
        value = attended[s] + rsd[s]
        rsd[s] = value
        sums.append(value)
        squares.append(value * value)
    both = squares[0] + squares[1]
    row = lax.broadcasted_iota(jnp.int32, (16, 128), 0)
    col = lax.broadcasted_iota(jnp.int32, (16, 128), 1)
    per_row = jnp.sum(both, axis=1, keepdims=True)
    sq0 = jnp.sum(per_row[0:8], axis=0, keepdims=True)
    sq1 = jnp.sum(per_row[8:16], axis=0, keepdims=True)
    square = jnp.where(row < 8, sq0, sq1)
    square_hi = square.astype(BF).astype(F32)
    square = jnp.where(col < 64, square_hi, square - square_hi)

    def pack_rows(index):
        return pl.ds(pl.multiple_of(index * 16, 16), 16)

    third = []
    for s in range(2):
        value = sums[s] * gpk[s]
        if s == 0:
            value = jnp.where(row % 8 == 7, square, value)
        region = recv3.at[s, pack_rows(there[s])]
        recv3[s, pack_rows(there[s]), :] = value.astype(BF)
        for k in range(1, 8):
            copy = remote(region, region, p3_ss.at[s, k], p3_rs.at[s, k], along(s, False, k))
            copy.start()
            third.append(copy)
    for copy in pending:
        copy.wait_send()

    normed = (n0, n1)

    def n_rows(core, index):
        return pl.ds(pl.multiple_of((core * 8 + index) * 16, 16), 16)

    fourth = []
    for s in range(2):
        for k in range(1, 8):
            landed(
                recv3.at[s, pack_rows((there[s] - k + 8) % 8)], p3_ss.at[s, k], p3_rs.at[s, k]
            )
        unp[s] = recv3[s].astype(F32)
        count = PAIRS + 1 - s
        rows = [
            jnp.concatenate(
                [unp[s, pl.ds(p * 8 + k, 8, stride=16), :] for k in range(count)], axis=1
            )
            for p in range(2)
        ]
        normed[s][n_rows(c, here[s]), :] = jnp.concatenate(rows, axis=0).astype(BF)
        region = normed[s].at[n_rows(c, here[s])]
        for k in range(1, 8):
            copy = remote(region, region, p4_ss.at[s, k], p4_rs.at[s, k], along(s, True, k))
            copy.start()
            fourth.append(copy)
        copy = remote(region, region, p5_ss.at[s, 0], p5_rs.at[s, 0], sibling)
        copy.start()
        fourth.append(copy)
    for copy in third:
        copy.wait_send()
    for k in range(1, 8):
        for s in range(2):
            region = normed[s].at[n_rows(c, (here[s] - k + 8) % 8)]
            landed(region, p4_ss.at[s, k], p4_rs.at[s, k])
            copy = remote(region, region, p5_ss.at[s, k], p5_rs.at[s, k], sibling)
            copy.start()
            fourth.append(copy)
    for k in range(8):
        for s in range(2):
            landed(
                normed[s].at[n_rows(sib, (here[s] - k + 8) % 8)], p5_ss.at[s, k], p5_rs.at[s, k]
            )

    part = dot(n0[:, 0:HALF], wc[0:HALF, :])
    part = part + swap_rows(dot(n1[...], wc[HALF : 2 * HALF, :]), perm)
    at = lax.broadcasted_iota(jnp.int32, (256, 128), 1)
    extra = part[:, 256:384]
    extra = jnp.where(at == 32, n0[:, HALF : HALF + 1].astype(F32), extra)
    extra = jnp.where(at == 33, n0[:, HALF + 64 : HALF + 65].astype(F32), extra)
    gs[:, 0:256] = part[:, 0:256].astype(BF)
    gs[:, 256:384] = extra.astype(BF)

    def quarter(index):
        return pl.ds(pl.multiple_of(index * 64, 64), 64)

    gx = []
    for k in range(1, 4):
        to = (t + k) % 4
        copy = remote(
            gs.at[quarter(to)], recvx.at[k], gx_ss.at[k], gx_rs.at[k], dev(Y, zc, to)
        )
        copy.start()
        gx.append(copy)
    for copy in fourth:
        copy.wait_send()
    value = gs[quarter(t), :].astype(F32)
    for k in range(1, 4):
        gx[k - 1].wait_recv()
        value = value + recvx[k].astype(F32)
    tail = value[:, 256:384]
    factor = lax.rsqrt((tail[:, 32:33] + tail[:, 33:34]) / D + EPS)
    up_tail = pltpu.roll(tail, 112, 1)

    def gated(gate, up):
        gate = gate * factor
        return gate / (1.0 + jnp.exp(-gate)) * (up * factor)

    column = lax.broadcasted_iota(jnp.int32, (64, 128), 1)
    hid[quarter(t), 0:128] = gated(value[:, 0:128], value[:, 128:256]).astype(BF)
    hid[quarter(t), 128:256] = jnp.where(
        column < 16, gated(jnp.where(column < 16, tail, 0.0), up_tail), 0.0
    ).astype(BF)
    hx = []
    region = hid.at[quarter(t)]
    for k in range(1, 4):
        copy = remote(region, region, hx_ss.at[k], hx_rs.at[k], dev(Y, zc, (t + k) % 4))
        copy.start()
        hx.append(copy)
    for copy in gx:
        copy.wait_send()
    for k in range(1, 4):
        landed(hid.at[quarter((t - k + 4) % 4)], hx_ss.at[k], hx_rs.at[k])
    a2[...] = swap_rows(hid[...].astype(F32), perm).astype(BF)
    for copy in hx:
        copy.wait_send()

    projected, pending = reduced(1, (hid, a2), wd)
    for s in range(2):
        value = rsd[s] + projected[s]
        for p in range(2):
            for k in range(PAIRS):
                n = s * PAIRS + k
                flat_row = value[p * 8 + k : p * 8 + k + 1, :]
                out_ref[0, p : p + 1, n * 128 : (n + 1) * 128] = flat_row.astype(BF)
    for copy in pending:
        copy.wait_send()
    hand.wait_send()


def body(
    cache, sent, slot_of, table, lengths, new_kv, queries, resid, gain, w_ov, w_gate, w_up, w_down
):
    smem = pl.BlockSpec(memory_space=pltpu.SMEM)
    vmem = pl.BlockSpec(memory_space=pltpu.VMEM)
    hbm = pl.BlockSpec(memory_space=pl.ANY)
    dma = pltpu.SemaphoreType.DMA
    scratch = [
        pltpu.VMEM((24, 64, 576), BF),
        pltpu.VMEM((4, 64, 576), BF),
        pltpu.VMEM((128, 576), BF),
        pltpu.VMEM((2, 64, 576), BF),
        pltpu.VMEM((256, 1792), BF),
        pltpu.VMEM((1792, 144), BF),
        pltpu.VMEM((1792, 144), BF),
        pltpu.VMEM((1792, 384), BF),
        pltpu.VMEM((256, 1792), BF),
        pltpu.VMEM((4, 2, 16, 640), BF),
        pltpu.VMEM((4, 2, 16, 640), BF),
        pltpu.VMEM((2, 16, 512), BF),
        pltpu.VMEM((8, 16, 512), BF),
        pltpu.VMEM((4, 128, 128), F32),
        pltpu.VMEM((2, 128, 256), BF),
        pltpu.VMEM((256, 256), BF),
        pltpu.VMEM((256, 256), BF),
        pltpu.VMEM((3, 256, 128), F32),
        pltpu.VMEM((2, 2, 128, HALF), BF),
        pltpu.VMEM((2, 2, 128, HALF), BF),
        pltpu.VMEM((2, 128, HALF), F32),
        pltpu.VMEM((2, 2, 128, HALF), BF),
        pltpu.VMEM((2, 2, 8, 16, HALF), BF),
        pltpu.VMEM((2, 128, 128), F32),
        pltpu.VMEM((2, 2, 128, 128), BF),
        pltpu.VMEM((2, 2, 8, 16, 128), BF),
        pltpu.VMEM((2, 16, 128), F32),
        pltpu.VMEM((2, 16, 128), F32),
        pltpu.VMEM((2, 128, 128), BF),
        pltpu.VMEM((2, 128, 128), F32),
        pltpu.VMEM((256, HALF + 128), BF),
        pltpu.VMEM((256, HALF), BF),
        pltpu.VMEM((256, 384), BF),
        pltpu.VMEM((4, 64, 384), BF),
        pltpu.VMEM((256, 256), BF),
        pltpu.VMEM((5, 128, 128), F32),
        dma((6,)),
        dma((2,)),
        dma((4,)),
        dma((4,)),
        dma((2,)),
        dma((2,)),
        dma((4,)),
        dma((4,)),
        dma((16,)),
        dma((16,)),
        dma((2, 2)),
        dma((2, 2)),
        dma((2, 2, 8)),
        dma((2, 2, 8)),
        dma((2, 2, 8)),
        dma((2, 2, 8)),
        dma((2, 8)),
        dma((2, 8)),
        dma((2, 8)),
        dma((2, 8)),
        dma((2, 8)),
        dma((2, 8)),
        dma((4,)),
        dma((4,)),
        dma((4,)),
        dma((4,)),
    ]
    return pl.pallas_call(
        kernel,
        out_shape=jax.ShapeDtypeStruct((1, 2, 1792), BF),
        in_specs=[smem, smem, smem, vmem, vmem, vmem] + [hbm] * 7,
        out_specs=vmem,
        scratch_shapes=scratch,
        compiler_params=pltpu.CompilerParams(
            collective_id=0, has_side_effects=True, vmem_limit_bytes=48 * 1024 * 1024
        ),
        cost_estimate=pl.CostEstimate(
            flops=2_000_000_000, bytes_accessed=6_000_000, transcendentals=250_000
        ),
    )(
        lengths,
        table,
        slot_of,
        new_kv,
        resid,
        gain.reshape(1, 1792),
        cache,
        sent,
        queries,
        w_ov,
        w_gate,
        w_up,
        w_down,
    )


def solution(mesh):
    in_specs = (
        P(("section", "dp"), "tp", None, None),
        P(("section", "dp"), "tp", None, None),
        P(("section", "dp"), "tp"),
        P(("section", "dp"), "tp"),
        P(("section", "dp")),
        P(("section", "dp"), None, None),
        P(("section", "dp"), None, None, None),
        P(("section", "dp"), None, "tp"),
        P("tp"),
        P(("section", "dp"), "tp"),
        P("tp", ("section", "dp")),
        P("tp", ("section", "dp")),
        P(("section", "dp"), "tp"),
    )
    out_specs = P(("section", "dp"), None, "tp")
    return jax.shard_map(body, mesh=mesh, in_specs=in_specs, out_specs=out_specs, check_vma=False)
```

```python
import functools

import jax
import jax.numpy as jnp
from jax import lax
from jax.experimental import pallas as pl
from jax.experimental.pallas import tpu as pltpu
from jax.sharding import PartitionSpec as P

D = 7168
LAT = 512
SCALE = 192.0 ** (-0.5)
EPS = 1e-06
LOW = -1e30
FLOOR = -1e20
MESH = pl.DeviceIdType.MESH
BF = jnp.bfloat16
F32 = jnp.float32
HALF = 896
PAIRS = 7

NT = (((1,), (1,)), ((), ()))


def dot(a, b):
    return jnp.dot(a, b, preferred_element_type=F32)


def dot_nt(a, b):
    return lax.dot_general(a, b, NT, preferred_element_type=F32)


def swap_rows(x, scratch):
    blocks = x.shape[1] // 128
    for c in range(2):
        for a in range(8):
            for p in range(2):
                row = c * 128 + a * 16 + p * 8
                for n in range(blocks):
                    scratch[n, pl.ds(c * 128 + p * 8 + a, 8, stride=16), :] = x[
                        row : row + 8, n * 128 : (n + 1) * 128
                    ]
    return jnp.concatenate([scratch[n] for n in range(blocks)], axis=1)


def kernel(
    lengths_ref,
    table_ref,
    slot_ref,
    new_ref,
    resid_ref,
    gain_ref,
    cache_ref,
    sent_ref,
    query_ref,
    wov_ref,
    wgate_ref,
    wup_ref,
    wdown_ref,
    out_ref,
    kv,
    kx,
    kn,
    qs,
    qx,
    qf,
    wov,
    wc,
    wd,
    l1s,
    l1r,
    zb,
    zr,
    lx,
    un,
    af,
    a1,
    a2,
    perm,
    core_send,
    core_recv,
    tot,
    send1,
    recv1,
    pack,
    send2,
    recv2,
    rsd,
    gpk,
    recv3,
    unp,
    n0,
    n1,
    gs,
    recvx,
    hid,
    flat,
    count,
    load_sem,
    q_ss,
    q_rs,
    l1_ss,
    l1_rs,
    lx_ss,
    lx_rs,
    lz_ss,
    lz_rs,
    core_ss,
    core_rs,
    p1_ss,
    p1_rs,
    p2_ss,
    p2_rs,
    p3_ss,
    p3_rs,
    p4_ss,
    p4_rs,
    p5_ss,
    p5_rs,
    gx_ss,
    gx_rs,
    hx_ss,
    hx_rs,
):
    dp = lax.axis_index("dp")
    t = lax.axis_index("tp")
    Y = lax.axis_index("section") * 4 + dp // 16
    zc = dp % 16
    z = zc // 2
    c = zc % 2
    sib = 1 - c

    def dev(y_, zc_, t_):
        return (y_ // 4, (y_ % 4) * 16 + zc_, t_)

    def along(s, first, k):
        if (s == 0) == first:
            return dev(Y, ((z + k) % 8) * 2 + c, t)
        return dev((Y + k) % 8, zc, t)

    here = (z, Y)
    there = (Y, z)
    sibling = dev(Y, z * 2 + sib, t)

    def remote(src, dst, ss, rs, to):
        return pltpu.make_async_remote_copy(
            src_ref=src, dst_ref=dst, send_sem=ss, recv_sem=rs, device_id=to, device_id_type=MESH
        )

    opened = []

    def send(src, dst, ss, rs, to):
        copy = remote(src, dst, ss, rs, to)
        copy.start()
        opened.append(copy)
        return copy

    def drain(count):
        for copy in opened[:count]:
            copy.wait_send()
        del opened[:count]

    def landed(region, ss, rs):
        remote(region, region, ss, rs, sibling).wait_recv()

    loads = [
        pltpu.make_async_copy(cache_ref.at[0], kv, load_sem.at[0]),
        pltpu.make_async_copy(query_ref.at[0], qs, load_sem.at[1]),
        pltpu.make_async_copy(wov_ref, wov, load_sem.at[2]),
        pltpu.make_async_copy(wgate_ref, wc.at[pl.ds(0, 144)], load_sem.at[3]),
        pltpu.make_async_copy(wup_ref, wc.at[pl.ds(144, 144)], load_sem.at[4]),
        pltpu.make_async_copy(wdown_ref, wd.at[pl.ds(0, 144)], load_sem.at[5]),
        pltpu.make_async_copy(sent_ref.at[0], kx, load_sem.at[6]),
        pltpu.make_async_copy(lengths_ref, count, load_sem.at[7]),
    ]
    for load in loads:
        load.start()

    waiting = dict(enumerate(loads))

    def loaded(n):
        waiting.pop(n).wait()

    def finish():
        drain(len(opened))
        for load in waiting.values():
            load.wait()
        out_ref[...] = jnp.zeros((1, 2, 1792), BF)

    barrier = pltpu.get_barrier_semaphore()
    for k in range(1, 8):
        pl.semaphore_signal(barrier, inc=1, device_id=dev((Y + k) % 8, zc, t), device_id_type=MESH)
    for k in range(1, 16):
        pl.semaphore_signal(barrier, inc=1, device_id=dev(Y, (zc + k) % 16, t), device_id_type=MESH)
    for k in range(1, 4):
        pl.semaphore_signal(barrier, inc=1, device_id=dev(Y, zc, (t + k) % 4), device_id_type=MESH)
    for j in range(2):
        for i in range(4):

            def greet():
                to = dev((Y + 16 - t - 4 * j) % 8, zc, i)
                pl.semaphore_signal(barrier, inc=1, device_id=to, device_id_type=MESH)

            if i == 0 and j == 0:
                pl.when(t != 0)(greet)
            else:
                greet()
    pl.semaphore_wait(barrier, jnp.where(t == 0, 32, 33))

    lane = lax.broadcasted_iota(jnp.int32, (1, 128), 1)
    loaded(7)
    length = count[0]
    late = [length - table_ref[0, slot_ref[0, e]] * 64 for e in range(4)]
    within = jnp.zeros((1, 128), jnp.int32)
    for e in range(4):
        within = jnp.where(lane == e, late[e], within)
    within = jnp.clip(within, 0, 64).astype(F32)
    loaded(1)
    q = qs[...].reshape(128, 576)
    qx[:, 0:512] = q[:, 0:512]
    qx[:, 512:640] = jnp.concatenate(
        [q[:, 512:576].astype(F32), jnp.broadcast_to(within[:, 0:64], (128, 64))], axis=1
    ).astype(BF)

    def q_rows(index):
        return pl.ds(pl.multiple_of(index * 32, 32), 32)

    first_q = send(
        qx.at[q_rows(t)], qf.at[q_rows(t)], q_ss.at[0], q_rs.at[0], dev((Y + 4) % 8, zc, t)
    )

    resid = resid_ref[0].astype(F32)
    for s in range(2):
        rsd[s] = jnp.zeros((16, 128), F32)
        gpk[s] = jnp.zeros((16, 128), F32)
        for p in range(2):
            for k in range(PAIRS):
                n = s * PAIRS + k
                rsd[s, p * 8 + k : p * 8 + k + 1, :] = resid[p : p + 1, n * 128 : (n + 1) * 128]
                gpk[s, p * 8 + k : p * 8 + k + 1, :] = gain_ref[n : n + 1, :]
    wd[pl.ds(144, 112)] = jnp.zeros((112, 1792), BF)
    kn[...] = jnp.zeros((128, 576), BF)
    kn[0:2, :] = new_ref[0]

    inside = lane % 64

    def bias_of(first, second):
        return jnp.where(inside < jnp.where(lane < 64, first, second), 0.0, LOW)

    limits = []
    for slot in range(24):
        limit = length - table_ref[0, slot] * 64
        for e in range(4):
            limit = jnp.where(slot_ref[0, e] == slot, 0, limit)
        limits.append(limit)
    bias = jnp.concatenate([bias_of(limits[i], limits[i + 1]) for i in range(0, 24, 2)], axis=1)
    head = lax.broadcasted_iota(jnp.int32, (128, 128), 0)
    entry = lax.broadcasted_iota(jnp.int32, (128, 128), 1)
    fresh = jnp.where(t == 0, 1, 0)
    bias_n = jnp.where(entry < jnp.where(head < 64, 1, 2) * fresh, 0.0, LOW)

    def partial(kind, q, chunks):
        scores = [dot_nt(q, keys) * SCALE + bias for keys, bias in chunks]
        top = functools.reduce(
            jnp.maximum, [jnp.max(score, axis=1, keepdims=True) for score in scores]
        )
        top = jnp.maximum(top, FLOOR)
        weights = [jnp.exp(score - top) for score in scores]
        total = functools.reduce(jnp.add, [jnp.sum(w, axis=1, keepdims=True) for w in weights])
        acc = functools.reduce(
            jnp.add, [dot(w.astype(BF), keys[:, :LAT]) for w, (keys, _) in zip(weights, chunks)]
        )
        total = jnp.where(total > 0.0, total, 1.0)
        acc = acc / total
        lse = top + jnp.log(total)
        hi = lse.astype(BF).astype(F32)
        mid = (lse - hi).astype(BF).astype(F32)
        low = lse - hi - mid
        for n in range(4):
            flat[kind, n] = acc[:, n * 128 : (n + 1) * 128]
        flat[kind, 4] = jnp.where(entry < 32, hi, jnp.where(entry < 64, mid, low))

    def spread(kind):
        for k in range(8):
            block = (Y + k) % 8
            rows = []
            for p in range(2):
                at = pl.ds(pl.multiple_of(p * 64 + block * 8, 8), 8)
                rows.append(jnp.concatenate([flat[kind, n, at, :] for n in range(5)], axis=1))
            l1s[kind, k] = jnp.concatenate(rows, axis=0).astype(BF)
            if k:
                send(
                    l1s.at[kind, k],
                    l1r.at[kind, k // 4, t],
                    l1_ss.at[kind, k],
                    l1_rs.at[kind, k // 4, t],
                    dev(block, zc, k % 4),
                )

        @pl.when(t == 0)
        def _():
            l1r[kind, 0, 0] = l1s[kind, 0]

        @pl.when(t != 0)
        def _():
            to_zero(kind).start()

    def to_zero(kind):
        return remote(
            l1s.at[kind, 0],
            l1r.at[kind, 0, t],
            l1_ss.at[kind, 0],
            l1_rs.at[kind, 0, t],
            dev(Y, zc, 0),
        )

    loaded(0)
    partial(0, q, [(kv[...].reshape(1536, 576), bias), (kn[...], bias_n)])

    landed(qf.at[q_rows(t)], q_ss.at[0], q_rs.at[0])
    region = qf.at[q_rows(t)]
    for k in range(1, 4):
        send(region, region, q_ss.at[k], q_rs.at[k], dev(Y, zc, (t + k) % 4))
    spread(0)
    drain(1)
    bounds = qf[q_rows(t), 512:640].astype(F32)[0:1, :]
    spot = inside.astype(F32)
    bias_x = jnp.concatenate(
        [
            jnp.where(
                spot < jnp.where(lane < 64, bounds[:, 64 + e : 65 + e], bounds[:, 65 + e : 66 + e]),
                0.0,
                LOW,
            )
            for e in (0, 2)
        ],
        axis=1,
    )
    loaded(6)
    for k in range(1, 4):
        landed(qf.at[q_rows((t - k + 4) % 4)], q_ss.at[k], q_rs.at[k])
    partial(1, qf[:, 0:576], [(kx[...].reshape(256, 576), bias_x)])
    spread(1)
    drain(3 + 7)

    def arrived(kind, j, i):
        def wait():
            landed(l1r.at[kind, j, i], l1_ss.at[kind, 0], l1_rs.at[kind, j, i])

        if i == 0 and j == 0:
            pl.when(t != 0)(wait)
        else:
            wait()

    for kind in range(2):
        for j in range(2):
            for i in range(4):
                arrived(kind, j, i)
    for j in range(2):
        parts = [
            l1r[kind, j ^ kind, i].astype(F32) for kind in range(2) for i in range(4)
        ]
        lses = [part[:, 512:513] + part[:, 544:545] + part[:, 576:577] for part in parts]
        best = functools.reduce(jnp.maximum, lses)
        shares = [jnp.exp(value - best) for value in lses]
        norm = functools.reduce(jnp.add, shares)
        mixed = functools.reduce(
            jnp.add, [part[:, :LAT] * share for part, share in zip(parts, shares)]
        )
        mixed = mixed / norm
        for p in range(2):
            for n in range(4):
                zb[n // 2, pl.ds(j * 4 + p * 2 + n % 2, 8, stride=8), :] = mixed[
                    p * 8 : p * 8 + 8, n * 128 : (n + 1) * 128
                ]

    def z_slot(zc_):
        return (zc_ % 2) * 8 + zc_ // 2

    for k in range(1, 16):
        to = (zc + k) % 16
        send(
            zb.at[to % 2, pl.ds(pl.multiple_of((to // 2) * 8, 8), 8)],
            zr.at[z_slot(zc)],
            lz_ss.at[k],
            lz_rs.at[k],
            dev(Y, to, t),
        )
    zr[z_slot(zc)] = zb[c, pl.ds(pl.multiple_of(z * 8, 8), 8), :]
    drain(7)

    @pl.when(t != 0)
    def _():
        to_zero(0).wait_send()
        to_zero(1).wait_send()

    loaded(2)
    loaded(3)
    loaded(4)
    loaded(5)
    for k in range(1, 16):
        landed(zr.at[z_slot((zc - k + 16) % 16)], lz_ss.at[k], lz_rs.at[k])
    lx[t] = zr[...].reshape(128, 128).astype(BF)
    for k in range(1, 4):
        send(lx.at[t], lx.at[t], lx_ss.at[k], lx_rs.at[k], dev(Y, zc, (t + k) % 4))
    drain(15)
    for k in range(4):
        source = (t - k + 4) % 4
        if k:
            landed(lx.at[source], lx_ss.at[k], lx_rs.at[k])
        un[k] = lx[source].astype(F32)
        for j in range(2):
            y_from = (Y - source - 4 * j + 8) % 8
            for p in range(2):
                for n in range(2):
                    for core in range(2):
                        rows = un[k, pl.ds(core * 64 + j * 4 + p * 2 + n, 8, stride=8), :]
                        af[0, n, pl.ds(core * 128 + p * 8 + y_from, 8, stride=16), :] = rows
                        at = pl.multiple_of(core * 128 + y_from * 16 + p * 8, 8)
                        af[1, n, pl.ds(at, 8), :] = rows
    a1[...] = jnp.concatenate([af[0, 0], af[0, 1]], axis=1).astype(BF)
    a2[...] = jnp.concatenate([af[1, 0], af[1, 1]], axis=1).astype(BF)
    drain(3)
    def reduced(u, operands, weight):
        before = len(opened)
        started = []
        for s in range(2):
            columns = slice(s * HALF, (s + 1) * HALF)
            rows = pl.ds(pl.multiple_of(sib * 128, 128), 128)
            core_send[u, s] = dot(operands[s][rows, :], weight[:, columns]).astype(BF)
            copy = send(
                core_send.at[u, s],
                core_recv.at[u, s],
                core_ss.at[u, s],
                core_rs.at[u, s],
                sibling,
            )
            started.append(copy)
        for s in range(2):
            columns = slice(s * HALF, (s + 1) * HALF)
            rows = pl.ds(pl.multiple_of(c * 128, 128), 128)
            tot[s] = dot(operands[s][rows, :], weight[:, columns])
        first = []
        for s in range(2):
            started[s].wait_recv()
            tot[s] = tot[s] + core_recv[u, s].astype(F32)
            send1[u, s] = tot[s].astype(BF)
            copies = []
            for k in range(1, 8):
                block = (here[s] + k) % 8
                copy = send(
                    send1.at[u, s, pl.ds(pl.multiple_of(block * 16, 16), 16)],
                    recv1.at[u, s, k],
                    p1_ss.at[u, s, k],
                    p1_rs.at[u, s, k],
                    along(s, True, k),
                )
                copies.append(copy)
            first.append(copies)
        drain(before + 2)
        second = []
        for s in range(2):
            part = tot[s, pl.ds(pl.multiple_of(here[s] * 16, 16), 16), :]
            for k in range(1, 8):
                first[s][k - 1].wait_recv()
                part = part + recv1[u, s, k].astype(F32)
            for p in range(2):
                for k in range(PAIRS):
                    pack[s, pl.ds(p * 8 + k, 8, stride=16), :] = part[
                        p * 8 : p * 8 + 8, k * 128 : (k + 1) * 128
                    ]
                pack[s, pl.ds(p * 8 + PAIRS, 8, stride=16), :] = jnp.zeros((8, 128), F32)
            send2[u, s] = pack[s].astype(BF)
            copies = []
            for k in range(1, 8):
                block = (there[s] + k) % 8
                copy = send(
                    send2.at[u, s, pl.ds(pl.multiple_of(block * 16, 16), 16)],
                    recv2.at[u, s, k],
                    p2_ss.at[u, s, k],
                    p2_rs.at[u, s, k],
                    along(s, False, k),
                )
                copies.append(copy)
            second.append(copies)
        drain(14)
        result = []
        for s in range(2):
            part = pack[s, pl.ds(pl.multiple_of(there[s] * 16, 16), 16), :]
            for k in range(1, 8):
                second[s][k - 1].wait_recv()
                part = part + recv2[u, s, k].astype(F32)
            result.append(part)
        return result

    attended = reduced(0, (a1, a2), wov)

    sums = []
    squares = []
    for s in range(2):
        value = attended[s] + rsd[s]
        rsd[s] = value
        sums.append(value)
        squares.append(value * value)
    both = squares[0] + squares[1]
    row = lax.broadcasted_iota(jnp.int32, (16, 128), 0)
    col = lax.broadcasted_iota(jnp.int32, (16, 128), 1)
    per_row = jnp.sum(both, axis=1, keepdims=True)
    sq0 = jnp.sum(per_row[0:8], axis=0, keepdims=True)
    sq1 = jnp.sum(per_row[8:16], axis=0, keepdims=True)
    square = jnp.where(row < 8, sq0, sq1)
    square_hi = square.astype(BF).astype(F32)
    square = jnp.where(col < 64, square_hi, square - square_hi)

    def pack_rows(index):
        return pl.ds(pl.multiple_of(index * 16, 16), 16)

    for s in range(2):
        value = sums[s] * gpk[s]
        if s == 0:
            value = jnp.where(row % 8 == 7, square, value)
        region = recv3.at[s, pack_rows(there[s])]
        recv3[s, pack_rows(there[s]), :] = value.astype(BF)
        for k in range(1, 8):
            send(region, region, p3_ss.at[s, k], p3_rs.at[s, k], along(s, False, k))
    drain(14)

    normed = (n0, n1)

    def n_rows(core, index):
        return pl.ds(pl.multiple_of((core * 8 + index) * 16, 16), 16)

    for s in range(2):
        for k in range(1, 8):
            landed(
                recv3.at[s, pack_rows((there[s] - k + 8) % 8)], p3_ss.at[s, k], p3_rs.at[s, k]
            )
        unp[s] = recv3[s].astype(F32)
        count = PAIRS + 1 - s
        rows = [
            jnp.concatenate(
                [unp[s, pl.ds(p * 8 + k, 8, stride=16), :] for k in range(count)], axis=1
            )
            for p in range(2)
        ]
        normed[s][n_rows(c, here[s]), :] = jnp.concatenate(rows, axis=0).astype(BF)
        region = normed[s].at[n_rows(c, here[s])]
        for k in range(1, 8):
            send(region, region, p4_ss.at[s, k], p4_rs.at[s, k], along(s, True, k))
        send(region, region, p5_ss.at[s, 0], p5_rs.at[s, 0], sibling)
    drain(14)
    for k in range(1, 8):
        for s in range(2):
            region = normed[s].at[n_rows(c, (here[s] - k + 8) % 8)]
            landed(region, p4_ss.at[s, k], p4_rs.at[s, k])
            send(region, region, p5_ss.at[s, k], p5_rs.at[s, k], sibling)
    for k in range(8):
        for s in range(2):
            landed(
                normed[s].at[n_rows(sib, (here[s] - k + 8) % 8)], p5_ss.at[s, k], p5_rs.at[s, k]
            )

    part = dot_nt(n0[:, 0:HALF], wc[:, 0:HALF])
    other = dot_nt(n1[...], wc[:, HALF : 2 * HALF])
    nothing = jnp.zeros((256, 96), F32)
    part = jnp.concatenate([part, nothing], axis=1)
    part = part + swap_rows(jnp.concatenate([other, nothing], axis=1), perm)
    at = lax.broadcasted_iota(jnp.int32, (256, 128), 1)
    extra = part[:, 256:384]
    extra = jnp.where(at == 32, n0[:, HALF : HALF + 1].astype(F32), extra)
    extra = jnp.where(at == 33, n0[:, HALF + 64 : HALF + 65].astype(F32), extra)
    gs[:, 0:256] = part[:, 0:256].astype(BF)
    gs[:, 256:384] = extra.astype(BF)

    def quarter(index):
        return pl.ds(pl.multiple_of(index * 64, 64), 64)

    gx = []
    for k in range(1, 4):
        to = (t + k) % 4
        gx.append(send(gs.at[quarter(to)], recvx.at[k], gx_ss.at[k], gx_rs.at[k], dev(Y, zc, to)))
    drain(30)
    value = gs[quarter(t), :].astype(F32)
    for k in range(1, 4):
        gx[k - 1].wait_recv()
        value = value + recvx[k].astype(F32)
    tail = value[:, 256:384]
    factor = lax.rsqrt((tail[:, 32:33] + tail[:, 33:34]) / D + EPS)
    ups = pltpu.roll(value, 240, 1)

    def gated(gate, up):
        gate = gate * factor
        return gate / (1.0 + jnp.exp(-gate)) * (up * factor)

    column = lax.broadcasted_iota(jnp.int32, (64, 256), 1)
    hid[quarter(t), :] = jnp.where(column < 144, gated(value[:, 0:256], ups[:, 0:256]), 0.0).astype(BF)
    region = hid.at[quarter(t)]
    for k in range(1, 4):
        send(region, region, hx_ss.at[k], hx_rs.at[k], dev(Y, zc, (t + k) % 4))
    drain(3)
    for k in range(1, 4):
        landed(hid.at[quarter((t - k + 4) % 4)], hx_ss.at[k], hx_rs.at[k])
    a2[...] = swap_rows(hid[...].astype(F32), perm).astype(BF)
    drain(3)

    projected = reduced(1, (hid, a2), wd)
    for s in range(2):
        value = rsd[s] + projected[s]
        for p in range(2):
            for k in range(PAIRS):
                n = s * PAIRS + k
                flat_row = value[p * 8 + k : p * 8 + k + 1, :]
                out_ref[0, p : p + 1, n * 128 : (n + 1) * 128] = flat_row.astype(BF)
    drain(len(opened))


def body(
    cache, sent, slot_of, table, lengths, new_kv, queries, resid, gain, w_ov, w_gate, w_up, w_down
):
    smem = pl.BlockSpec(memory_space=pltpu.SMEM)
    vmem = pl.BlockSpec(memory_space=pltpu.VMEM)
    hbm = pl.BlockSpec(memory_space=pl.ANY)
    dma = pltpu.SemaphoreType.DMA
    scratch = [
        pltpu.VMEM((24, 64, 576), BF),
        pltpu.VMEM((4, 64, 576), BF),
        pltpu.VMEM((128, 576), BF),
        pltpu.VMEM((2, 64, 576), BF),
        pltpu.VMEM((128, 640), BF),
        pltpu.VMEM((128, 640), BF),
        pltpu.VMEM((256, 1792), BF),
        pltpu.VMEM((288, 1792), BF),
        pltpu.VMEM((256, 1792), BF),
        pltpu.VMEM((2, 8, 16, 640), BF),
        pltpu.VMEM((2, 2, 4, 16, 640), BF),
        pltpu.VMEM((2, 64, 128), F32),
        pltpu.VMEM((16, 8, 128), F32),
        pltpu.VMEM((4, 128, 128), BF),
        pltpu.VMEM((4, 128, 128), F32),
        pltpu.VMEM((2, 2, 256, 128), F32),
        pltpu.VMEM((256, 256), BF),
        pltpu.VMEM((256, 256), BF),
        pltpu.VMEM((3, 256, 128), F32),
        pltpu.VMEM((2, 2, 128, HALF), BF),
        pltpu.VMEM((2, 2, 128, HALF), BF),
        pltpu.VMEM((2, 128, HALF), F32),
        pltpu.VMEM((2, 2, 128, HALF), BF),
        pltpu.VMEM((2, 2, 8, 16, HALF), BF),
        pltpu.VMEM((2, 128, 128), F32),
        pltpu.VMEM((2, 2, 128, 128), BF),
        pltpu.VMEM((2, 2, 8, 16, 128), BF),
        pltpu.VMEM((2, 16, 128), F32),
        pltpu.VMEM((2, 16, 128), F32),
        pltpu.VMEM((2, 128, 128), BF),
        pltpu.VMEM((2, 128, 128), F32),
        pltpu.VMEM((256, HALF + 128), BF),
        pltpu.VMEM((256, HALF), BF),
        pltpu.VMEM((256, 384), BF),
        pltpu.VMEM((4, 64, 384), BF),
        pltpu.VMEM((256, 256), BF),
        pltpu.VMEM((2, 5, 128, 128), F32),
        pltpu.SMEM((1,), jnp.int32),
        dma((8,)),
        dma((4,)),
        dma((4,)),
        dma((2, 8)),
        dma((2, 2, 4)),
        dma((4,)),
        dma((4,)),
        dma((16,)),
        dma((16,)),
        dma((2, 2)),
        dma((2, 2)),
        dma((2, 2, 8)),
        dma((2, 2, 8)),
        dma((2, 2, 8)),
        dma((2, 2, 8)),
        dma((2, 8)),
        dma((2, 8)),
        dma((2, 8)),
        dma((2, 8)),
        dma((2, 8)),
        dma((2, 8)),
        dma((4,)),
        dma((4,)),
        dma((4,)),
        dma((4,)),
    ]
    return pl.pallas_call(
        kernel,
        out_shape=jax.ShapeDtypeStruct((1, 2, 1792), BF),
        in_specs=[pl.BlockSpec(memory_space=pltpu.HBM), smem, smem, vmem, vmem, vmem] + [hbm] * 7,
        out_specs=vmem,
        scratch_shapes=scratch,
        compiler_params=pltpu.CompilerParams(
            collective_id=0, has_side_effects=True, vmem_limit_bytes=60 * 1024 * 1024
        ),
        cost_estimate=pl.CostEstimate(
            flops=2_000_000_000, bytes_accessed=6_000_000, transcendentals=250_000
        ),
    )(
        lengths,
        table,
        slot_of,
        new_kv,
        resid,
        gain.reshape(14, 128),
        cache,
        sent,
        queries,
        w_ov,
        w_gate.T,
        w_up.T,
        w_down,
    )


def solution(mesh):
    in_specs = (
        P(("section", "dp"), "tp", None, None),
        P(("section", "dp"), "tp", None, None),
        P(("section", "dp"), "tp"),
        P(("section", "dp"), "tp"),
        P(("section", "dp")),
        P(("section", "dp"), None, None),
        P(("section", "dp"), None, None, None),
        P(("section", "dp"), None, "tp"),
        P("tp"),
        P(("section", "dp"), "tp"),
        P("tp", ("section", "dp")),
        P("tp", ("section", "dp")),
        P(("section", "dp"), "tp"),
    )
    out_specs = P(("section", "dp"), None, "tp")
    return jax.shard_map(body, mesh=mesh, in_specs=in_specs, out_specs=out_specs, check_vma=False)
```

```python
import functools

import jax
import jax.numpy as jnp
from jax import lax
from jax.experimental import pallas as pl
from jax.experimental.pallas import tpu as pltpu
from jax.sharding import PartitionSpec as P

D = 7168
LAT = 512
SCALE = 192.0 ** (-0.5)
EPS = 1e-06
LOW = -1e30
FLOOR = -1e20
MESH = pl.DeviceIdType.MESH
BF = jnp.bfloat16
F32 = jnp.float32
HALF = 896
PAIRS = 7

NT = (((1,), (1,)), ((), ()))
RING = (4, 3, 5, 2, 6, 1, 7)


def dot(a, b):
    return jnp.dot(a, b, preferred_element_type=F32)


def dot_nt(a, b):
    return lax.dot_general(a, b, NT, preferred_element_type=F32)


def swap_rows(x, scratch, core):
    blocks = x.shape[1] // 128
    start = core * 128
    for a in range(8):
        for p in range(2):
            row = a * 16 + p * 8
            for n in range(blocks):
                scratch[n, pl.ds(start + p * 8 + a, 8, stride=16), :] = x[
                    row : row + 8, n * 128 : (n + 1) * 128
                ]
    return jnp.concatenate([scratch[n, start : start + 128, :] for n in range(blocks)], axis=1)


def kernel(
    lengths_ref,
    table_ref,
    slot_ref,
    new_ref,
    resid_ref,
    gain_ref,
    cache_ref,
    sent_ref,
    query_ref,
    wov_ref,
    wgate_ref,
    wup_ref,
    wdown_ref,
    out_ref,
    kv,
    kx,
    kn,
    qs,
    qx,
    qf,
    wov,
    wc,
    wd,
    l1s,
    l1r,
    zb,
    zs,
    zt,
    lx,
    un,
    af,
    a1,
    a2,
    perm,
    core_send,
    core_recv,
    tot,
    send1,
    recv1,
    pack,
    send2,
    recv2,
    rsd,
    gpk,
    recv3,
    unp,
    n0,
    n1,
    gs,
    recvx,
    hid,
    flat,
    numbers,
    slots,
    newest,
    base,
    gains,
    load_sem,
    q_ss,
    q_rs,
    l1_ss,
    l1_rs,
    lx_ss,
    lx_rs,
    lz_ss,
    lz_rs,
    core_ss,
    core_rs,
    p1_ss,
    p1_rs,
    p2_ss,
    p2_rs,
    p3_ss,
    p3_rs,
    p4_ss,
    p4_rs,
    p5_ss,
    p5_rs,
    gx_ss,
    gx_rs,
    hx_ss,
    hx_rs,
):
    dp = lax.axis_index("dp")
    t = lax.axis_index("tp")
    Y = lax.axis_index("section") * 4 + dp // 16
    zc = dp % 16
    z = zc // 2
    c = zc % 2
    sib = 1 - c

    def dev(y_, zc_, t_):
        return (y_ // 4, (y_ % 4) * 16 + zc_, t_)

    def along(s, first, k):
        if (s == 0) == first:
            return dev(Y, ((z + k) % 8) * 2 + c, t)
        return dev((Y + k) % 8, zc, t)

    here = (z, Y)
    there = (Y, z)
    sibling = dev(Y, z * 2 + sib, t)

    def remote(src, dst, ss, rs, to):
        return pltpu.make_async_remote_copy(
            src_ref=src, dst_ref=dst, send_sem=ss, recv_sem=rs, device_id=to, device_id_type=MESH
        )

    opened = []

    def send(src, dst, ss, rs, to):
        copy = remote(src, dst, ss, rs, to)
        copy.start()
        opened.append(copy)
        return copy

    def drain(count):
        for copy in opened[:count]:
            copy.wait_send()
        del opened[:count]

    def landed(region, ss, rs):
        remote(region, region, ss, rs, sibling).wait_recv()

    loads = [
        pltpu.make_async_copy(cache_ref.at[0], kv, load_sem.at[0]),
        pltpu.make_async_copy(query_ref.at[0], qs, load_sem.at[1]),
        pltpu.make_async_copy(wov_ref, wov, load_sem.at[2]),
        pltpu.make_async_copy(wgate_ref, wc.at[pl.ds(0, 144)], load_sem.at[3]),
        pltpu.make_async_copy(wup_ref, wc.at[pl.ds(144, 144)], load_sem.at[4]),
        pltpu.make_async_copy(wdown_ref, wd.at[pl.ds(0, 144)], load_sem.at[5]),
        pltpu.make_async_copy(sent_ref.at[0], kx, load_sem.at[6]),
        pltpu.make_async_copy(table_ref, numbers, load_sem.at[7]),
        pltpu.make_async_copy(slot_ref, slots, load_sem.at[8]),
        pltpu.make_async_copy(new_ref, newest, load_sem.at[9]),
        pltpu.make_async_copy(resid_ref, base, load_sem.at[10]),
        pltpu.make_async_copy(gain_ref, gains, load_sem.at[11]),
    ]
    for load in loads:
        load.start()

    waiting = dict(enumerate(loads))

    def loaded(n):
        waiting.pop(n).wait()

    def finish():
        drain(len(opened))
        for load in waiting.values():
            load.wait()
        out_ref[...] = jnp.zeros((1, 2, 1792), BF)

    barrier = pltpu.get_barrier_semaphore()
    for k in RING:
        pl.semaphore_signal(barrier, inc=1, device_id=dev((Y + k) % 8, zc, t), device_id_type=MESH)
    for k in range(1, 4):
        pl.semaphore_signal(barrier, inc=1, device_id=dev(Y, zc, (t + k) % 4), device_id_type=MESH)
    for j in range(2):
        for i in range(4):

            def greet():
                to = dev((Y + 16 - t - 4 * j) % 8, zc, i)
                pl.semaphore_signal(barrier, inc=1, device_id=to, device_id_type=MESH)

            if i == 0 and j == 0:
                pl.when(t != 0)(greet)
            else:
                greet()
    for k in RING:
        to = dev(Y, ((z + k) % 8) * 2 + c, t)
        pl.semaphore_signal(barrier, inc=1, device_id=to, device_id_type=MESH)
    pl.semaphore_signal(barrier, inc=1, device_id=sibling, device_id_type=MESH)
    pl.semaphore_wait(barrier, jnp.where(t == 0, 25, 26))

    lane = lax.broadcasted_iota(jnp.int32, (1, 128), 1)
    loaded(7)
    loaded(8)
    length = lengths_ref[0, 0]
    late = [length - numbers[0, slots[0, e]] * 64 for e in range(4)]
    within = jnp.zeros((1, 128), jnp.int32)
    for e in range(4):
        within = jnp.where(lane == e, late[e], within)
    within = jnp.clip(within, 0, 64).astype(F32)
    loaded(1)
    q = qs[...].reshape(128, 576)
    qx[:, 0:512] = q[:, 0:512]
    qx[:, 512:640] = jnp.concatenate(
        [q[:, 512:576].astype(F32), jnp.broadcast_to(within[:, 0:64], (128, 64))], axis=1
    ).astype(BF)

    def q_rows(index):
        return pl.ds(pl.multiple_of(index * 32, 32), 32)

    first_q = send(
        qx.at[q_rows(t)], qf.at[q_rows(t)], q_ss.at[0], q_rs.at[0], dev((Y + 4) % 8, zc, t)
    )

    loaded(9)
    loaded(10)
    loaded(11)
    resid = base[0].astype(F32)
    for s in range(2):
        rsd[s] = jnp.zeros((16, 128), F32)
        gpk[s] = jnp.zeros((16, 128), F32)
        for p in range(2):
            for k in range(PAIRS):
                n = s * PAIRS + k
                rsd[s, p * 8 + k : p * 8 + k + 1, :] = resid[p : p + 1, n * 128 : (n + 1) * 128]
                gpk[s, p * 8 + k : p * 8 + k + 1, :] = gains[n : n + 1, :]
    wd[pl.ds(144, 112)] = jnp.zeros((112, 1792), BF)
    kn[...] = jnp.zeros((128, 576), BF)
    kn[0:2, :] = newest[0]

    inside = lane % 64

    def bias_of(first, second):
        return jnp.where(inside < jnp.where(lane < 64, first, second), 0.0, LOW)

    limits = []
    for slot in range(24):
        limit = length - numbers[0, slot] * 64
        for e in range(4):
            limit = jnp.where(slots[0, e] == slot, 0, limit)
        limits.append(limit)
    bias = jnp.concatenate([bias_of(limits[i], limits[i + 1]) for i in range(0, 24, 2)], axis=1)
    head = lax.broadcasted_iota(jnp.int32, (128, 128), 0)
    entry = lax.broadcasted_iota(jnp.int32, (128, 128), 1)
    fresh = jnp.where(t == 0, 1, 0)
    bias_n = jnp.where(entry < jnp.where(head < 64, 1, 2) * fresh, 0.0, LOW)

    def partial(kind, q, chunks):
        scores = [dot_nt(q, keys) * SCALE + bias for keys, bias in chunks]
        top = functools.reduce(
            jnp.maximum, [jnp.max(score, axis=1, keepdims=True) for score in scores]
        )
        top = jnp.maximum(top, FLOOR)
        weights = [jnp.exp(score - top) for score in scores]
        total = functools.reduce(jnp.add, [jnp.sum(w, axis=1, keepdims=True) for w in weights])
        acc = functools.reduce(
            jnp.add, [dot(w.astype(BF), keys[:, :LAT]) for w, (keys, _) in zip(weights, chunks)]
        )
        total = jnp.where(total > 0.0, total, 1.0)
        acc = acc / total
        lse = top + jnp.log(total)
        hi = lse.astype(BF).astype(F32)
        mid = (lse - hi).astype(BF).astype(F32)
        low = lse - hi - mid
        for n in range(4):
            flat[kind, n] = acc[:, n * 128 : (n + 1) * 128]
        flat[kind, 4] = jnp.where(entry < 32, hi, jnp.where(entry < 64, mid, low))

    def spread(kind):
        for k in RING + (0,):
            block = (Y + k) % 8
            rows = []
            for p in range(2):
                at = pl.ds(pl.multiple_of(p * 64 + block * 8, 8), 8)
                rows.append(jnp.concatenate([flat[kind, n, at, :] for n in range(5)], axis=1))
            l1s[kind, k] = jnp.concatenate(rows, axis=0).astype(BF)
            if k:
                send(
                    l1s.at[kind, k],
                    l1r.at[kind, k // 4, t],
                    l1_ss.at[kind, k],
                    l1_rs.at[kind, k // 4, t],
                    dev(block, zc, k % 4),
                )

        @pl.when(t == 0)
        def _():
            l1r[kind, 0, 0] = l1s[kind, 0]

        @pl.when(t != 0)
        def _():
            to_zero(kind).start()

    def to_zero(kind):
        return remote(
            l1s.at[kind, 0],
            l1r.at[kind, 0, t],
            l1_ss.at[kind, 0],
            l1_rs.at[kind, 0, t],
            dev(Y, zc, 0),
        )

    loaded(0)
    partial(0, q, [(kv[...].reshape(1536, 576), bias), (kn[...], bias_n)])

    spread(0)

    landed(qf.at[q_rows(t)], q_ss.at[0], q_rs.at[0])
    region = qf.at[q_rows(t)]
    for k in range(1, 4):
        send(region, region, q_ss.at[k], q_rs.at[k], dev(Y, zc, (t + k) % 4))
    drain(8)
    bounds = qf[q_rows(t), 512:640].astype(F32)[0:1, :]
    spot = inside.astype(F32)
    bias_x = jnp.concatenate(
        [
            jnp.where(
                spot < jnp.where(lane < 64, bounds[:, 64 + e : 65 + e], bounds[:, 65 + e : 66 + e]),
                0.0,
                LOW,
            )
            for e in (0, 2)
        ],
        axis=1,
    )
    loaded(6)
    for k in range(1, 4):
        landed(qf.at[q_rows((t - k + 4) % 4)], q_ss.at[k], q_rs.at[k])

    partial(1, qf[:, 0:576], [(kx[...].reshape(256, 576), bias_x)])
    spread(1)
    drain(3)

    def arrived(kind, j, i):
        def wait():
            landed(l1r.at[kind, j, i], l1_ss.at[kind, 0], l1_rs.at[kind, j, i])

        if i == 0 and j == 0:
            pl.when(t != 0)(wait)
        else:
            wait()

    def joined(parts):
        best = functools.reduce(jnp.maximum, [part[0] for part in parts])
        shares = [jnp.exp(part[0] - best) for part in parts]
        norm = functools.reduce(jnp.add, [part[1] * w for part, w in zip(parts, shares)])
        mixed = functools.reduce(jnp.add, [part[2] * w for part, w in zip(parts, shares)])
        return best, norm, mixed

    def parts_of(kind, j):
        found = []
        for i in range(4):
            part = l1r[kind, j, i].astype(F32)
            lse = part[:, 512:513] + part[:, 544:545] + part[:, 576:577]
            found.append((lse, 1.0, part[:, :LAT]))
        return found

    for j in range(2):
        for i in range(4):
            arrived(0, j, i)
    early = [joined(parts_of(0, j)) for j in range(2)]
    for j in range(2):
        for i in range(4):
            arrived(1, j, i)
    for j in range(2):
        _, norm, mixed = joined([early[j]] + parts_of(1, 1 - j))
        mixed = mixed / norm
        for p in range(2):
            for n in range(4):
                zb[n // 2, pl.ds(j * 4 + p * 2 + n % 2, 8, stride=8), :] = mixed[
                    p * 8 : p * 8 + 8, n * 128 : (n + 1) * 128
                ]

    halves = remote(zb.at[sib], zs, lz_ss.at[0], lz_rs.at[0], sibling)
    halves.start()
    drain(7)

    @pl.when(t != 0)
    def _():
        to_zero(0).wait_send()
        to_zero(1).wait_send()

    own_half = zb[c]
    halves.wait_recv()
    sib_half = zs[...]
    lower = jnp.where(c == 0, own_half, sib_half)
    upper = jnp.where(c == 0, sib_half, own_half)
    for a in range(8):
        rows = slice(a * 8, a * 8 + 8)
        zt[a] = jnp.concatenate([lower[rows], upper[rows]], axis=0).astype(BF)
    for k in RING:
        to = (z + k) % 8
        send(zt.at[to], lx.at[t, z], lz_ss.at[k], lz_rs.at[k], dev(Y, to * 2 + c, t))
    lx[t, z] = zt[z]
    halves.wait_send()
    loaded(2)
    loaded(3)
    loaded(4)
    loaded(5)
    for k in range(1, 8):
        landed(lx.at[t, (z - k + 8) % 8], lz_ss.at[k], lz_rs.at[k])
    for k in range(1, 4):
        send(lx.at[t], lx.at[t], lx_ss.at[k], lx_rs.at[k], dev(Y, zc, (t + k) % 4))
    drain(7)
    for k in range(4):
        source = (t - k + 4) % 4
        if k:
            landed(lx.at[source], lx_ss.at[k], lx_rs.at[k])
        un[k] = lx[source].reshape(128, 128).astype(F32)
        for j in range(2):
            y_from = (Y - source - 4 * j + 8) % 8
            for p in range(2):
                for n in range(2):
                    for core in range(2):
                        rows = un[k, pl.ds(core * 8 + j * 4 + p * 2 + n, 8, stride=16), :]
                        af[0, n, pl.ds(core * 128 + p * 8 + y_from, 8, stride=16), :] = rows
                        at = pl.multiple_of(core * 128 + y_from * 16 + p * 8, 8)
                        af[1, n, pl.ds(at, 8), :] = rows
    a1[...] = jnp.concatenate([af[0, 0], af[0, 1]], axis=1).astype(BF)
    a2[...] = jnp.concatenate([af[1, 0], af[1, 1]], axis=1).astype(BF)
    drain(3)
    def core_copy(u, s):
        return remote(
            core_send.at[u, s], core_recv.at[u, s], core_ss.at[u, s], core_rs.at[u, s], sibling
        )

    def first_copy(u, s, k):
        block = (here[s] + k) % 8
        return remote(
            send1.at[u, s, pl.ds(pl.multiple_of(block * 16, 16), 16)],
            recv1.at[u, s, k],
            p1_ss.at[u, s, k],
            p1_rs.at[u, s, k],
            along(s, True, k),
        )

    def start_first(u):
        for s in range(2):
            core_copy(u, s).wait_recv()
            total = tot[s] + core_recv[u, s].astype(F32)
            tot[s] = total
            send1[u, s] = total.astype(BF)
            for k in RING:
                first_copy(u, s, k).start()

    def rest(u):
        for s in range(2):
            core_copy(u, s).wait_send()
        second = []
        for s in range(2):
            part = tot[s, pl.ds(pl.multiple_of(here[s] * 16, 16), 16), :]
            for k in range(1, 8):
                first_copy(u, s, k).wait_recv()
                part = part + recv1[u, s, k].astype(F32)
            for p in range(2):
                for k in range(PAIRS):
                    pack[s, pl.ds(p * 8 + k, 8, stride=16), :] = part[
                        p * 8 : p * 8 + 8, k * 128 : (k + 1) * 128
                    ]
                pack[s, pl.ds(p * 8 + PAIRS, 8, stride=16), :] = jnp.zeros((8, 128), F32)
            send2[u, s] = pack[s].astype(BF)
            copies = {}
            for k in RING:
                block = (there[s] + k) % 8
                copy = send(
                    send2.at[u, s, pl.ds(pl.multiple_of(block * 16, 16), 16)],
                    recv2.at[u, s, k],
                    p2_ss.at[u, s, k],
                    p2_rs.at[u, s, k],
                    along(s, False, k),
                )
                copies[k] = copy
            second.append(copies)
        for s in range(2):
            for k in range(1, 8):
                first_copy(u, s, k).wait_send()
        result = []
        for s in range(2):
            part = pack[s, pl.ds(pl.multiple_of(there[s] * 16, 16), 16), :]
            for k in range(1, 8):
                second[s][k].wait_recv()
                part = part + recv2[u, s, k].astype(F32)
            result.append(part)
        return result

    for s in range(2):
        columns = slice(s * HALF, (s + 1) * HALF)
        rows = pl.ds(pl.multiple_of(sib * 128, 128), 128)
        core_send[0, s] = dot((a1, a2)[s][rows, :], wov[:, columns]).astype(BF)
        core_copy(0, s).start()
    for s in range(2):
        columns = slice(s * HALF, (s + 1) * HALF)
        rows = pl.ds(pl.multiple_of(c * 128, 128), 128)
        tot[s] = dot((a1, a2)[s][rows, :], wov[:, columns])
    start_first(0)
    attended = rest(0)

    sums = []
    squares = []
    for s in range(2):
        value = attended[s] + rsd[s]
        rsd[s] = value
        sums.append(value)
        squares.append(value * value)
    both = squares[0] + squares[1]
    row = lax.broadcasted_iota(jnp.int32, (16, 128), 0)
    col = lax.broadcasted_iota(jnp.int32, (16, 128), 1)
    per_row = jnp.sum(both, axis=1, keepdims=True)
    sq0 = jnp.sum(per_row[0:8], axis=0, keepdims=True)
    sq1 = jnp.sum(per_row[8:16], axis=0, keepdims=True)
    square = jnp.where(row < 8, sq0, sq1)
    square_hi = square.astype(BF).astype(F32)
    square = jnp.where(col < 64, square_hi, square - square_hi)

    def pack_rows(index):
        return pl.ds(pl.multiple_of(index * 16, 16), 16)

    for s in range(2):
        value = sums[s] * gpk[s]
        if s == 0:
            value = jnp.where(row % 8 == 7, square, value)
        region = recv3.at[s, pack_rows(there[s])]
        recv3[s, pack_rows(there[s]), :] = value.astype(BF)
        for k in RING:
            send(region, region, p3_ss.at[s, k], p3_rs.at[s, k], along(s, False, k))
    drain(14)

    normed = (n0, n1)

    def n_rows(core, index):
        return pl.ds(pl.multiple_of((core * 8 + index) * 16, 16), 16)

    for s in range(2):
        for k in range(1, 8):
            landed(
                recv3.at[s, pack_rows((there[s] - k + 8) % 8)], p3_ss.at[s, k], p3_rs.at[s, k]
            )
        unp[s] = recv3[s].astype(F32)
        count = PAIRS + 1 - s
        rows = [
            jnp.concatenate(
                [unp[s, pl.ds(p * 8 + k, 8, stride=16), :] for k in range(count)], axis=1
            )
            for p in range(2)
        ]
        normed[s][n_rows(c, here[s]), :] = jnp.concatenate(rows, axis=0).astype(BF)
        region = normed[s].at[n_rows(c, here[s])]
        for k in RING:
            send(region, region, p4_ss.at[s, k], p4_rs.at[s, k], along(s, True, k))
        send(region, region, p5_ss.at[s, 0], p5_rs.at[s, 0], sibling)
    drain(14)
    for k in (1, 7, 2, 6, 3, 5, 4):
        for s in range(2):
            region = normed[s].at[n_rows(c, (here[s] - k + 8) % 8)]
            landed(region, p4_ss.at[s, k], p4_rs.at[s, k])
            send(region, region, p5_ss.at[s, k], p5_rs.at[s, k], sibling)
    for k in range(8):
        for s in range(2):
            landed(
                normed[s].at[n_rows(sib, (here[s] - k + 8) % 8)], p5_ss.at[s, k], p5_rs.at[s, k]
            )

    nothing = jnp.zeros((128, 96), F32)
    at = lax.broadcasted_iota(jnp.int32, (128, 128), 1)
    column = lax.broadcasted_iota(jnp.int32, (32, 256), 1)

    def quarter(core, index):
        return pl.ds(pl.multiple_of(core * 128 + index * 32, 32), 32)

    def products(core):
        rows = slice(core * 128, (core + 1) * 128)
        part = jnp.concatenate([dot_nt(n0[rows, 0:HALF], wc[:, 0:HALF]), nothing], axis=1)
        other = jnp.concatenate([dot_nt(n1[rows, :], wc[:, HALF : 2 * HALF]), nothing], axis=1)
        part = part + swap_rows(other, perm, core)
        extra = part[:, 256:384]
        extra = jnp.where(at == 32, n0[rows, HALF : HALF + 1].astype(F32), extra)
        extra = jnp.where(at == 33, n0[rows, HALF + 64 : HALF + 65].astype(F32), extra)
        gs[rows, 0:256] = part[:, 0:256].astype(BF)
        gs[rows, 256:384] = extra.astype(BF)
        for k in range(1, 4):
            to = (t + k) % 4
            send(
                gs.at[quarter(core, to)],
                recvx.at[core, k],
                gx_ss.at[core, k],
                gx_rs.at[core, k],
                dev(Y, zc, to),
            )

    def gates(core):
        value = gs[quarter(core, t), :].astype(F32)
        for k in range(1, 4):
            landed(recvx.at[core, k], gx_ss.at[core, k], gx_rs.at[core, k])
            value = value + recvx[core, k].astype(F32)
        tail = value[:, 256:384]
        factor = lax.rsqrt((tail[:, 32:33] + tail[:, 33:34]) / D + EPS)
        gate = value[:, 0:256] * factor
        up = pltpu.roll(value, 240, 1)[:, 0:256] * factor
        done = jnp.where(column < 144, gate / (1.0 + jnp.exp(-gate)) * up, 0.0)
        hid[quarter(core, t), :] = done.astype(BF)
        region = hid.at[quarter(core, t)]
        for k in range(1, 4):
            send(region, region, hx_ss.at[core, k], hx_rs.at[core, k], dev(Y, zc, (t + k) % 4))

    def down(core):
        for k in range(1, 4):
            landed(
                hid.at[quarter(core, (t - k + 4) % 4)], hx_ss.at[core, k], hx_rs.at[core, k]
            )
        rows = hid[core * 128 : (core + 1) * 128, :]
        turned = swap_rows(rows.astype(F32), perm, core).astype(BF)
        for s in range(2):
            term = dot((rows, turned)[s], wd[:, s * HALF : (s + 1) * HALF])

            @pl.when(c == core)
            def _():
                tot[s] = term

            @pl.when(c != core)
            def _():
                core_send[1, s] = term.astype(BF)
                core_copy(1, s).start()

    products(0)
    products(1)
    drain(30)
    gates(0)
    gates(1)
    down(0)

    @pl.when(c == 0)
    def _():
        start_first(1)

    down(1)

    @pl.when(c == 1)
    def _():
        start_first(1)

    drain(12)
    projected = rest(1)
    for s in range(2):
        value = rsd[s] + projected[s]
        for p in range(2):
            for k in range(PAIRS):
                n = s * PAIRS + k
                flat_row = value[p * 8 + k : p * 8 + k + 1, :]
                out_ref[0, p : p + 1, n * 128 : (n + 1) * 128] = flat_row.astype(BF)
    drain(len(opened))


def body(
    cache, sent, slot_of, table, lengths, new_kv, queries, resid, gain, w_ov, w_gate, w_up, w_down
):
    smem = pl.BlockSpec(memory_space=pltpu.SMEM)
    vmem = pl.BlockSpec(memory_space=pltpu.VMEM)
    hbm = pl.BlockSpec(memory_space=pl.ANY)
    dma = pltpu.SemaphoreType.DMA
    scratch = [
        pltpu.VMEM((24, 64, 576), BF),
        pltpu.VMEM((4, 64, 576), BF),
        pltpu.VMEM((128, 576), BF),
        pltpu.VMEM((2, 64, 576), BF),
        pltpu.VMEM((128, 640), BF),
        pltpu.VMEM((128, 640), BF),
        pltpu.VMEM((256, 1792), BF),
        pltpu.VMEM((288, 1792), BF),
        pltpu.VMEM((256, 1792), BF),
        pltpu.VMEM((2, 8, 16, 640), BF),
        pltpu.VMEM((2, 2, 4, 16, 640), BF),
        pltpu.VMEM((2, 64, 128), F32),
        pltpu.VMEM((64, 128), F32),
        pltpu.VMEM((8, 16, 128), BF),
        pltpu.VMEM((4, 8, 16, 128), BF),
        pltpu.VMEM((4, 128, 128), F32),
        pltpu.VMEM((2, 2, 256, 128), F32),
        pltpu.VMEM((256, 256), BF),
        pltpu.VMEM((256, 256), BF),
        pltpu.VMEM((3, 256, 128), F32),
        pltpu.VMEM((2, 2, 128, HALF), BF),
        pltpu.VMEM((2, 2, 128, HALF), BF),
        pltpu.VMEM((2, 128, HALF), F32),
        pltpu.VMEM((2, 2, 128, HALF), BF),
        pltpu.VMEM((2, 2, 8, 16, HALF), BF),
        pltpu.VMEM((2, 128, 128), F32),
        pltpu.VMEM((2, 2, 128, 128), BF),
        pltpu.VMEM((2, 2, 8, 16, 128), BF),
        pltpu.VMEM((2, 16, 128), F32),
        pltpu.VMEM((2, 16, 128), F32),
        pltpu.VMEM((2, 128, 128), BF),
        pltpu.VMEM((2, 128, 128), F32),
        pltpu.VMEM((256, HALF + 128), BF),
        pltpu.VMEM((256, HALF), BF),
        pltpu.VMEM((256, 384), BF),
        pltpu.VMEM((2, 4, 32, 384), BF),
        pltpu.VMEM((256, 256), BF),
        pltpu.VMEM((2, 5, 128, 128), F32),
        pltpu.SMEM((1, 24), jnp.int32),
        pltpu.SMEM((1, 4), jnp.int32),
        pltpu.VMEM((1, 2, 576), BF),
        pltpu.VMEM((1, 2, 1792), BF),
        pltpu.VMEM((14, 128), F32),
        dma((12,)),
        dma((4,)),
        dma((4,)),
        dma((2, 8)),
        dma((2, 2, 4)),
        dma((4,)),
        dma((4,)),
        dma((8,)),
        dma((8,)),
        dma((2, 2)),
        dma((2, 2)),
        dma((2, 2, 8)),
        dma((2, 2, 8)),
        dma((2, 2, 8)),
        dma((2, 2, 8)),
        dma((2, 8)),
        dma((2, 8)),
        dma((2, 8)),
        dma((2, 8)),
        dma((2, 8)),
        dma((2, 8)),
        dma((2, 4)),
        dma((2, 4)),
        dma((2, 4)),
        dma((2, 4)),
    ]
    return pl.pallas_call(
        kernel,
        out_shape=jax.ShapeDtypeStruct((1, 2, 1792), BF),
        in_specs=[smem] + [hbm] * 12,
        out_specs=vmem,
        scratch_shapes=scratch,
        compiler_params=pltpu.CompilerParams(
            collective_id=0, has_side_effects=True, vmem_limit_bytes=60 * 1024 * 1024
        ),
        cost_estimate=pl.CostEstimate(
            flops=2_000_000_000, bytes_accessed=6_000_000, transcendentals=250_000
        ),
    )(
        lengths.reshape(1, 1),
        table,
        slot_of,
        new_kv,
        resid,
        gain.reshape(14, 128),
        cache,
        sent,
        queries,
        w_ov,
        w_gate.T,
        w_up.T,
        w_down,
    )


def solution(mesh):
    in_specs = (
        P(("section", "dp"), "tp", None, None),
        P(("section", "dp"), "tp", None, None),
        P(("section", "dp"), "tp"),
        P(("section", "dp"), "tp"),
        P(("section", "dp")),
        P(("section", "dp"), None, None),
        P(("section", "dp"), None, None, None),
        P(("section", "dp"), None, "tp"),
        P("tp"),
        P(("section", "dp"), "tp"),
        P("tp", ("section", "dp")),
        P("tp", ("section", "dp")),
        P(("section", "dp"), "tp"),
    )
    out_specs = P(("section", "dp"), None, "tp")
    return jax.shard_map(body, mesh=mesh, in_specs=in_specs, out_specs=out_specs, check_vma=False)
```

```python
import functools

import jax
import jax.numpy as jnp
from jax import lax
from jax.experimental import pallas as pl
from jax.experimental.pallas import tpu as pltpu
from jax.sharding import PartitionSpec as P

D = 7168
LAT = 512
SCALE = 192.0 ** (-0.5)
EPS = 1e-06
LOW = -1e30
FLOOR = -1e20
MESH = pl.DeviceIdType.MESH
BF = jnp.bfloat16
F32 = jnp.float32
HALF = 896
PAIRS = 7

NT = (((1,), (1,)), ((), ()))
ROUND = (2, 1, 3)
RING = (4, 3, 5, 2, 6, 1, 7)
TURNS = RING + (0,)


def dot(a, b):
    return jnp.dot(a, b, preferred_element_type=F32)


def dot_nt(a, b):
    return lax.dot_general(a, b, NT, preferred_element_type=F32)


def swap_rows(x, scratch, core):
    blocks = x.shape[1] // 128
    start = core * 128
    for a in range(8):
        for p in range(2):
            row = a * 16 + p * 8
            for n in range(blocks):
                scratch[n, pl.ds(start + p * 8 + a, 8, stride=16), :] = x[
                    row : row + 8, n * 128 : (n + 1) * 128
                ]
    return jnp.concatenate([scratch[n, start : start + 128, :] for n in range(blocks)], axis=1)


def kernel(
    lengths_ref,
    table_ref,
    slot_ref,
    new_ref,
    resid_ref,
    gain_ref,
    cache_ref,
    sent_ref,
    query_ref,
    wov_ref,
    wgate_ref,
    wup_ref,
    wdown_ref,
    out_ref,
    kv,
    kx,
    kn,
    qs,
    qx,
    qf,
    wov,
    wc,
    wd,
    l1s,
    l1r,
    zb,
    zs,
    zt,
    lx,
    un,
    af,
    a1,
    a2,
    perm,
    core_send,
    core_recv,
    tot,
    send1,
    recv1,
    pack,
    send2,
    recv2,
    rsd,
    gpk,
    recv3,
    unp,
    n0,
    n1,
    gs,
    recvx,
    hid,
    flat,
    numbers,
    slots,
    newest,
    base,
    gains,
    count,
    load_sem,
    q_ss,
    q_rs,
    l1_ss,
    l1_rs,
    lx_ss,
    lx_rs,
    lz_ss,
    lz_rs,
    core_ss,
    core_rs,
    p1_ss,
    p1_rs,
    p2_ss,
    p2_rs,
    p3_ss,
    p3_rs,
    p4_ss,
    p4_rs,
    p5_ss,
    p5_rs,
    gx_ss,
    gx_rs,
    hx_ss,
    hx_rs,
):
    dp = lax.axis_index("dp")
    t = lax.axis_index("tp")
    Y = lax.axis_index("section") * 4 + dp // 16
    zc = dp % 16
    z = zc // 2
    c = zc % 2
    sib = 1 - c

    def dev(y_, zc_, t_):
        return (y_ // 4, (y_ % 4) * 16 + zc_, t_)

    def along(s, first, k):
        if (s == 0) == first:
            return dev(Y, ((z + k) % 8) * 2 + c, t)
        return dev((Y + k) % 8, zc, t)

    here = (z, Y)
    there = (Y, z)
    sibling = dev(Y, z * 2 + sib, t)

    def remote(src, dst, ss, rs, to):
        return pltpu.make_async_remote_copy(
            src_ref=src, dst_ref=dst, send_sem=ss, recv_sem=rs, device_id=to, device_id_type=MESH
        )

    opened = []

    def send(src, dst, ss, rs, to):
        copy = remote(src, dst, ss, rs, to)
        copy.start()
        opened.append(copy)
        return copy

    def drain(count):
        for copy in opened[:count]:
            copy.wait_send()
        del opened[:count]

    def landed(region, ss, rs):
        remote(region, region, ss, rs, sibling).wait_recv()

    loads = [
        pltpu.make_async_copy(cache_ref.at[0], kv, load_sem.at[0]),
        pltpu.make_async_copy(query_ref.at[0], qs, load_sem.at[1]),
        pltpu.make_async_copy(wov_ref, wov, load_sem.at[2]),
        pltpu.make_async_copy(wgate_ref, wc.at[pl.ds(0, 144)], load_sem.at[3]),
        pltpu.make_async_copy(wup_ref, wc.at[pl.ds(144, 144)], load_sem.at[4]),
        pltpu.make_async_copy(wdown_ref, wd.at[pl.ds(0, 144)], load_sem.at[5]),
        pltpu.make_async_copy(sent_ref.at[0], kx, load_sem.at[6]),
        pltpu.make_async_copy(table_ref, numbers, load_sem.at[7]),
        pltpu.make_async_copy(slot_ref, slots, load_sem.at[8]),
        pltpu.make_async_copy(new_ref, newest, load_sem.at[9]),
        pltpu.make_async_copy(resid_ref, base, load_sem.at[10]),
        pltpu.make_async_copy(gain_ref, gains, load_sem.at[11]),
        pltpu.make_async_copy(lengths_ref, count, load_sem.at[12]),
    ]

    waiting = dict(enumerate(loads))

    def loaded(n):
        waiting.pop(n).wait()

    barrier = pltpu.get_barrier_semaphore()
    for k in RING:
        pl.semaphore_signal(barrier, inc=1, device_id=dev((Y + k) % 8, zc, t), device_id_type=MESH)
    for k in range(1, 4):
        pl.semaphore_signal(barrier, inc=1, device_id=dev(Y, zc, (t + k) % 4), device_id_type=MESH)
    for j in range(2):
        for i in range(4):

            def greet():
                to = dev((Y + 16 - t - 4 * j) % 8, zc, i)
                pl.semaphore_signal(barrier, inc=1, device_id=to, device_id_type=MESH)

            if i == 0 and j == 0:
                pl.when(t != 0)(greet)
            else:
                greet()
    for k in RING:
        to = dev(Y, ((z + k) % 8) * 2 + c, t)
        pl.semaphore_signal(barrier, inc=1, device_id=to, device_id_type=MESH)
    pl.semaphore_signal(barrier, inc=1, device_id=sibling, device_id_type=MESH)
    for n in (1, 7, 8, 12):
        loads[n].start()
    pl.semaphore_wait(barrier, jnp.where(t == 0, 25, 26))

    lane = lax.broadcasted_iota(jnp.int32, (1, 128), 1)
    loaded(7)
    loaded(8)
    loaded(12)
    length = count[0, 0]
    late = [length - numbers[0, slots[0, e]] * 64 for e in range(4)]
    within = jnp.zeros((1, 128), jnp.int32)
    for e in range(4):
        within = jnp.where(lane == e, late[e], within)
    within = jnp.clip(within, 0, 64).astype(F32)
    loaded(1)
    q = qs[...].reshape(128, 576)
    qx[:, 0:512] = q[:, 0:512]
    qx[:, 512:640] = jnp.concatenate(
        [q[:, 512:576].astype(F32), jnp.broadcast_to(within[:, 0:64], (128, 64))], axis=1
    ).astype(BF)

    def q_rows(index):
        return pl.ds(pl.multiple_of(index * 32, 32), 32)

    first_q = send(
        qx.at[q_rows(t)], qf.at[q_rows(t)], q_ss.at[0], q_rs.at[0], dev((Y + 4) % 8, zc, t)
    )

    for n in (0, 6, 9, 10, 11, 2, 3, 4, 5):
        loads[n].start()

    loaded(9)
    loaded(10)
    loaded(11)
    resid = base[0].astype(F32)
    for s in range(2):
        rsd[s] = jnp.zeros((16, 128), F32)
        gpk[s] = jnp.zeros((16, 128), F32)
        for p in range(2):
            for k in range(PAIRS):
                n = s * PAIRS + k
                rsd[s, p * 8 + k : p * 8 + k + 1, :] = resid[p : p + 1, n * 128 : (n + 1) * 128]
                gpk[s, p * 8 + k : p * 8 + k + 1, :] = gains[n : n + 1, :]
    wd[pl.ds(144, 112)] = jnp.zeros((112, 1792), BF)
    kn[...] = jnp.zeros((128, 576), BF)
    kn[0:2, :] = newest[0]

    inside = lane % 64

    def bias_of(first, second):
        return jnp.where(inside < jnp.where(lane < 64, first, second), 0.0, LOW)

    limits = []
    for slot in range(24):
        limit = length - numbers[0, slot] * 64
        for e in range(4):
            limit = jnp.where(slots[0, e] == slot, 0, limit)
        limits.append(limit)
    bias = jnp.concatenate([bias_of(limits[i], limits[i + 1]) for i in range(0, 24, 2)], axis=1)
    head = lax.broadcasted_iota(jnp.int32, (128, 128), 0)
    entry = lax.broadcasted_iota(jnp.int32, (128, 128), 1)
    fresh = jnp.where(t == 0, 1, 0)
    bias_n = jnp.where(entry < jnp.where(head < 64, 1, 2) * fresh, 0.0, LOW)

    def partial(kind, q, chunks):
        scores = [dot_nt(q, keys) * SCALE + bias for keys, bias in chunks]
        top = functools.reduce(
            jnp.maximum, [jnp.max(score, axis=1, keepdims=True) for score in scores]
        )
        top = jnp.maximum(top, FLOOR)
        weights = [jnp.exp(score - top) for score in scores]
        total = functools.reduce(jnp.add, [jnp.sum(w, axis=1, keepdims=True) for w in weights])
        acc = functools.reduce(
            jnp.add, [dot(w.astype(BF), keys[:, :LAT]) for w, (keys, _) in zip(weights, chunks)]
        )
        total = jnp.where(total > 0.0, total, 1.0)
        acc = acc / total
        lse = top + jnp.log(total)
        hi = lse.astype(BF).astype(F32)
        mid = (lse - hi).astype(BF).astype(F32)
        low = lse - hi - mid
        for n in range(4):
            flat[kind, n] = acc[:, n * 128 : (n + 1) * 128]
        flat[kind, 4] = jnp.where(entry < 32, hi, jnp.where(entry < 64, mid, low))

    def spread(kind):
        for k in RING + (0,):
            block = (Y + k) % 8
            rows = []
            for p in range(2):
                at = pl.ds(pl.multiple_of(p * 64 + block * 8, 8), 8)
                rows.append(jnp.concatenate([flat[kind, n, at, :] for n in range(5)], axis=1))
            l1s[kind, k] = jnp.concatenate(rows, axis=0).astype(BF)
            if k:
                send(
                    l1s.at[kind, k],
                    l1r.at[kind, k // 4, t],
                    l1_ss.at[kind, k],
                    l1_rs.at[kind, k // 4, t],
                    dev(block, zc, k % 4),
                )

        @pl.when(t == 0)
        def _():
            l1r[kind, 0, 0] = l1s[kind, 0]

        @pl.when(t != 0)
        def _():
            to_zero(kind).start()

    def to_zero(kind):
        return remote(
            l1s.at[kind, 0],
            l1r.at[kind, 0, t],
            l1_ss.at[kind, 0],
            l1_rs.at[kind, 0, t],
            dev(Y, zc, 0),
        )

    loaded(0)
    partial(0, q, [(kv[...].reshape(1536, 576), bias), (kn[...], bias_n)])

    spread(0)

    landed(qf.at[q_rows(t)], q_ss.at[0], q_rs.at[0])
    region = qf.at[q_rows(t)]
    for k in ROUND:
        send(region, region, q_ss.at[k], q_rs.at[k], dev(Y, zc, (t + k) % 4))
    drain(8)
    bounds = qf[q_rows(t), 512:640].astype(F32)[0:1, :]
    spot = inside.astype(F32)
    bias_x = jnp.concatenate(
        [
            jnp.where(
                spot < jnp.where(lane < 64, bounds[:, 64 + e : 65 + e], bounds[:, 65 + e : 66 + e]),
                0.0,
                LOW,
            )
            for e in (0, 2)
        ],
        axis=1,
    )
    loaded(6)
    for k in range(1, 4):
        landed(qf.at[q_rows((t - k + 4) % 4)], q_ss.at[k], q_rs.at[k])

    partial(1, qf[:, 0:576], [(kx[...].reshape(256, 576), bias_x)])
    spread(1)
    drain(3)

    def arrived(kind, j, i):
        def wait():
            landed(l1r.at[kind, j, i], l1_ss.at[kind, 0], l1_rs.at[kind, j, i])

        if i == 0 and j == 0:
            pl.when(t != 0)(wait)
        else:
            wait()

    def joined(parts):
        best = functools.reduce(jnp.maximum, [part[0] for part in parts])
        shares = [jnp.exp(part[0] - best) for part in parts]
        norm = functools.reduce(jnp.add, [part[1] * w for part, w in zip(parts, shares)])
        mixed = functools.reduce(jnp.add, [part[2] * w for part, w in zip(parts, shares)])
        return best, norm, mixed

    def parts_of(kind, j):
        found = []
        for i in range(4):
            part = l1r[kind, j, i].astype(F32)
            lse = part[:, 512:513] + part[:, 544:545] + part[:, 576:577]
            found.append((lse, 1.0, part[:, :LAT]))
        return found

    for j in range(2):
        for i in range(4):
            arrived(0, j, i)
    early = [joined(parts_of(0, j)) for j in range(2)]
    for j in range(2):
        for i in range(4):
            arrived(1, j, i)
    for j in range(2):
        _, norm, mixed = joined([early[j]] + parts_of(1, 1 - j))
        mixed = mixed / norm
        for p in range(2):
            for n in range(4):
                zb[n // 2, pl.ds(j * 4 + p * 2 + n % 2, 8, stride=8), :] = mixed[
                    p * 8 : p * 8 + 8, n * 128 : (n + 1) * 128
                ]

    halves = remote(zb.at[sib], zs, lz_ss.at[0], lz_rs.at[0], sibling)
    halves.start()
    drain(7)

    @pl.when(t != 0)
    def _():
        to_zero(0).wait_send()
        to_zero(1).wait_send()

    own_half = zb[c]
    halves.wait_recv()
    sib_half = zs[...]
    lower = jnp.where(c == 0, own_half, sib_half)
    upper = jnp.where(c == 0, sib_half, own_half)
    for a in range(8):
        rows = slice(a * 8, a * 8 + 8)
        zt[a] = jnp.concatenate([lower[rows], upper[rows]], axis=0).astype(BF)
    for k in RING:
        to = (z + k) % 8
        send(zt.at[to], lx.at[t, z], lz_ss.at[k], lz_rs.at[k], dev(Y, to * 2 + c, t))
    lx[t, z] = zt[z]
    halves.wait_send()
    loaded(2)
    loaded(3)
    loaded(4)
    loaded(5)
    for k in range(1, 8):
        landed(lx.at[t, (z - k + 8) % 8], lz_ss.at[k], lz_rs.at[k])
    for k in ROUND:
        send(lx.at[t], lx.at[t], lx_ss.at[k], lx_rs.at[k], dev(Y, zc, (t + k) % 4))
    drain(7)
    for k in range(4):
        source = (t - k + 4) % 4
        if k:
            landed(lx.at[source], lx_ss.at[k], lx_rs.at[k])
        un[k] = lx[source].reshape(128, 128).astype(F32)
        for j in range(2):
            y_from = (Y - source - 4 * j + 8) % 8
            for p in range(2):
                for n in range(2):
                    for core in range(2):
                        rows = un[k, pl.ds(core * 8 + j * 4 + p * 2 + n, 8, stride=16), :]
                        af[0, n, pl.ds(core * 128 + p * 8 + y_from, 8, stride=16), :] = rows
                        at = pl.multiple_of(core * 128 + y_from * 16 + p * 8, 8)
                        af[1, n, pl.ds(at, 8), :] = rows
    a1[...] = jnp.concatenate([af[0, 0], af[0, 1]], axis=1).astype(BF)
    a2[...] = jnp.concatenate([af[1, 0], af[1, 1]], axis=1).astype(BF)
    drain(3)
    def core_copy(u, s, part):
        region = (u, s, pl.ds(part * 64, 64))
        return remote(
            core_send.at[region],
            core_recv.at[region],
            core_ss.at[u, s, part],
            core_rs.at[u, s, part],
            sibling,
        )

    def first_copy(u, s, k):
        return remote(
            send1.at[u, s, pl.ds(TURNS.index(k) * 16, 16)],
            recv1.at[u, s, k],
            p1_ss.at[u, s, k],
            p1_rs.at[u, s, k],
            along(s, True, k),
        )

    def half_rows(source, s, core, part):
        blocks = []
        for k in TURNS[part * 4 : part * 4 + 4]:
            at = pl.multiple_of(core * 128 + ((here[s] + k) % 8) * 16, 16)
            blocks.append(source[pl.ds(at, 16), :])
        return jnp.concatenate(blocks, axis=0)

    def start_first(u):
        for part in range(2):
            rows = slice(part * 64, part * 64 + 64)
            for s in range(2):
                core_copy(u, s, part).wait_recv()
                total = tot[s, rows, :] + core_recv[u, s, rows, :].astype(F32)
                tot[s, rows, :] = total
                send1[u, s, rows, :] = total.astype(BF)
                for k in TURNS[part * 4 : part * 4 + 4]:
                    if k:
                        first_copy(u, s, k).start()

    def rest(u):
        for s in range(2):
            for part in range(2):
                core_copy(u, s, part).wait_send()
        second = []
        for s in range(2):
            part = tot[s, 112:128, :]
            for k in range(1, 8):
                first_copy(u, s, k).wait_recv()
                part = part + recv1[u, s, k].astype(F32)
            for p in range(2):
                for k in range(PAIRS):
                    pack[s, pl.ds(p * 8 + k, 8, stride=16), :] = part[
                        p * 8 : p * 8 + 8, k * 128 : (k + 1) * 128
                    ]
                pack[s, pl.ds(p * 8 + PAIRS, 8, stride=16), :] = jnp.zeros((8, 128), F32)
            send2[u, s] = pack[s].astype(BF)
            copies = {}
            for k in RING:
                block = (there[s] + k) % 8
                copy = send(
                    send2.at[u, s, pl.ds(pl.multiple_of(block * 16, 16), 16)],
                    recv2.at[u, s, k],
                    p2_ss.at[u, s, k],
                    p2_rs.at[u, s, k],
                    along(s, False, k),
                )
                copies[k] = copy
            second.append(copies)
        for s in range(2):
            for k in range(1, 8):
                first_copy(u, s, k).wait_send()
        result = []
        for s in range(2):
            part = pack[s, pl.ds(pl.multiple_of(there[s] * 16, 16), 16), :]
            for k in range(1, 8):
                second[s][k].wait_recv()
                part = part + recv2[u, s, k].astype(F32)
            result.append(part)
        return result

    for part in range(2):
        for s in range(2):
            rows = slice(part * 64, part * 64 + 64)
            columns = slice(s * HALF, (s + 1) * HALF)
            term = dot(half_rows((a1, a2)[s], s, sib, part), wov[:, columns])
            core_send[0, s, rows, :] = term.astype(BF)
            core_copy(0, s, part).start()
    for s in range(2):
        columns = slice(s * HALF, (s + 1) * HALF)
        whole = [half_rows((a1, a2)[s], s, c, part) for part in range(2)]
        tot[s] = dot(jnp.concatenate(whole, axis=0), wov[:, columns])
    start_first(0)
    attended = rest(0)

    sums = []
    squares = []
    for s in range(2):
        value = attended[s] + rsd[s]
        rsd[s] = value
        sums.append(value)
        squares.append(value * value)
    both = squares[0] + squares[1]
    row = lax.broadcasted_iota(jnp.int32, (16, 128), 0)
    col = lax.broadcasted_iota(jnp.int32, (16, 128), 1)
    per_row = jnp.sum(both, axis=1, keepdims=True)
    sq0 = jnp.sum(per_row[0:8], axis=0, keepdims=True)
    sq1 = jnp.sum(per_row[8:16], axis=0, keepdims=True)
    square = jnp.where(row < 8, sq0, sq1)
    square_hi = square.astype(BF).astype(F32)
    square = jnp.where(col < 64, square_hi, square - square_hi)

    def pack_rows(index):
        return pl.ds(pl.multiple_of(index * 16, 16), 16)

    for s in range(2):
        value = sums[s] * gpk[s]
        if s == 0:
            value = jnp.where(row % 8 == 7, square, value)
        region = recv3.at[s, pack_rows(there[s])]
        recv3[s, pack_rows(there[s]), :] = value.astype(BF)
        for k in RING:
            send(region, region, p3_ss.at[s, k], p3_rs.at[s, k], along(s, False, k))
    drain(14)

    normed = (n0, n1)

    def n_rows(core, index):
        return pl.ds(pl.multiple_of((core * 8 + index) * 16, 16), 16)

    for s in range(2):
        for k in range(1, 8):
            landed(
                recv3.at[s, pack_rows((there[s] - k + 8) % 8)], p3_ss.at[s, k], p3_rs.at[s, k]
            )
        unp[s] = recv3[s].astype(F32)
        count = PAIRS + 1 - s
        rows = [
            jnp.concatenate(
                [unp[s, pl.ds(p * 8 + k, 8, stride=16), :] for k in range(count)], axis=1
            )
            for p in range(2)
        ]
        normed[s][n_rows(c, here[s]), :] = jnp.concatenate(rows, axis=0).astype(BF)
        region = normed[s].at[n_rows(c, here[s])]
        for k in RING:
            send(region, region, p4_ss.at[s, k], p4_rs.at[s, k], along(s, True, k))
        send(region, region, p5_ss.at[s, 0], p5_rs.at[s, 0], sibling)
    drain(14)
    for k in (1, 7, 2, 6, 3, 5, 4):
        for s in range(2):
            region = normed[s].at[n_rows(c, (here[s] - k + 8) % 8)]
            landed(region, p4_ss.at[s, k], p4_rs.at[s, k])
            send(region, region, p5_ss.at[s, k], p5_rs.at[s, k], sibling)
    for k in range(8):
        for s in range(2):
            landed(
                normed[s].at[n_rows(sib, (here[s] - k + 8) % 8)], p5_ss.at[s, k], p5_rs.at[s, k]
            )

    nothing = jnp.zeros((128, 96), F32)
    at = lax.broadcasted_iota(jnp.int32, (128, 128), 1)
    column = lax.broadcasted_iota(jnp.int32, (32, 256), 1)

    def quarter(core, index):
        return pl.ds(pl.multiple_of(core * 128 + index * 32, 32), 32)

    def products(core):
        rows = slice(core * 128, (core + 1) * 128)
        part = jnp.concatenate([dot_nt(n0[rows, 0:HALF], wc[:, 0:HALF]), nothing], axis=1)
        other = jnp.concatenate([dot_nt(n1[rows, :], wc[:, HALF : 2 * HALF]), nothing], axis=1)
        part = part + swap_rows(other, perm, core)
        extra = part[:, 256:384]
        extra = jnp.where(at == 32, n0[rows, HALF : HALF + 1].astype(F32), extra)
        extra = jnp.where(at == 33, n0[rows, HALF + 64 : HALF + 65].astype(F32), extra)
        gs[rows, 0:256] = part[:, 0:256].astype(BF)
        gs[rows, 256:384] = extra.astype(BF)
        for k in ROUND:
            to = (t + k) % 4
            send(
                gs.at[quarter(core, to)],
                recvx.at[core, k],
                gx_ss.at[core, k],
                gx_rs.at[core, k],
                dev(Y, zc, to),
            )

    def gates(core):
        value = gs[quarter(core, t), :].astype(F32)
        for k in range(1, 4):
            landed(recvx.at[core, k], gx_ss.at[core, k], gx_rs.at[core, k])
            value = value + recvx[core, k].astype(F32)
        tail = value[:, 256:384]
        factor = lax.rsqrt((tail[:, 32:33] + tail[:, 33:34]) / D + EPS)
        gate = value[:, 0:256] * factor
        up = pltpu.roll(value, 240, 1)[:, 0:256] * factor
        done = jnp.where(column < 144, gate / (1.0 + jnp.exp(-gate)) * up, 0.0)
        hid[quarter(core, t), :] = done.astype(BF)
        region = hid.at[quarter(core, t)]
        for k in ROUND:
            send(region, region, hx_ss.at[core, k], hx_rs.at[core, k], dev(Y, zc, (t + k) % 4))

    def down(core):
        for k in range(1, 4):
            landed(
                hid.at[quarter(core, (t - k + 4) % 4)], hx_ss.at[core, k], hx_rs.at[core, k]
            )
        rows = hid[core * 128 : (core + 1) * 128, :]
        a2[core * 128 : (core + 1) * 128, :] = swap_rows(rows.astype(F32), perm, core).astype(BF)
        for part in range(2):
            for s in range(2):
                rows = slice(part * 64, part * 64 + 64)
                columns = slice(s * HALF, (s + 1) * HALF)
                term = dot(half_rows((hid, a2)[s], s, core, part), wd[:, columns])

                @pl.when(c == core)
                def _():
                    tot[s, rows, :] = term

                @pl.when(c != core)
                def _():
                    core_send[1, s, rows, :] = term.astype(BF)
                    core_copy(1, s, part).start()

    products(0)
    products(1)
    drain(30)
    gates(0)
    gates(1)
    down(0)

    @pl.when(c == 0)
    def _():
        start_first(1)

    down(1)

    @pl.when(c == 1)
    def _():
        start_first(1)

    drain(12)
    projected = rest(1)
    for s in range(2):
        value = rsd[s] + projected[s]
        for p in range(2):
            for k in range(PAIRS):
                n = s * PAIRS + k
                flat_row = value[p * 8 + k : p * 8 + k + 1, :]
                out_ref[0, p : p + 1, n * 128 : (n + 1) * 128] = flat_row.astype(BF)
    drain(len(opened))


def body(
    cache, sent, slot_of, table, lengths, new_kv, queries, resid, gain, w_ov, w_gate, w_up, w_down
):
    vmem = pl.BlockSpec(memory_space=pltpu.VMEM)
    hbm = pl.BlockSpec(memory_space=pl.ANY)
    dma = pltpu.SemaphoreType.DMA
    scratch = [
        pltpu.VMEM((24, 64, 576), BF),
        pltpu.VMEM((4, 64, 576), BF),
        pltpu.VMEM((128, 576), BF),
        pltpu.VMEM((2, 64, 576), BF),
        pltpu.VMEM((128, 640), BF),
        pltpu.VMEM((128, 640), BF),
        pltpu.VMEM((256, 1792), BF),
        pltpu.VMEM((288, 1792), BF),
        pltpu.VMEM((256, 1792), BF),
        pltpu.VMEM((2, 8, 16, 640), BF),
        pltpu.VMEM((2, 2, 4, 16, 640), BF),
        pltpu.VMEM((2, 64, 128), F32),
        pltpu.VMEM((64, 128), F32),
        pltpu.VMEM((8, 16, 128), BF),
        pltpu.VMEM((4, 8, 16, 128), BF),
        pltpu.VMEM((4, 128, 128), F32),
        pltpu.VMEM((2, 2, 256, 128), F32),
        pltpu.VMEM((256, 256), BF),
        pltpu.VMEM((256, 256), BF),
        pltpu.VMEM((3, 256, 128), F32),
        pltpu.VMEM((2, 2, 128, HALF), BF),
        pltpu.VMEM((2, 2, 128, HALF), BF),
        pltpu.VMEM((2, 128, HALF), F32),
        pltpu.VMEM((2, 2, 128, HALF), BF),
        pltpu.VMEM((2, 2, 8, 16, HALF), BF),
        pltpu.VMEM((2, 128, 128), F32),
        pltpu.VMEM((2, 2, 128, 128), BF),
        pltpu.VMEM((2, 2, 8, 16, 128), BF),
        pltpu.VMEM((2, 16, 128), F32),
        pltpu.VMEM((2, 16, 128), F32),
        pltpu.VMEM((2, 128, 128), BF),
        pltpu.VMEM((2, 128, 128), F32),
        pltpu.VMEM((256, HALF + 128), BF),
        pltpu.VMEM((256, HALF), BF),
        pltpu.VMEM((256, 384), BF),
        pltpu.VMEM((2, 4, 32, 384), BF),
        pltpu.VMEM((256, 256), BF),
        pltpu.VMEM((2, 5, 128, 128), F32),
        pltpu.SMEM((1, 24), jnp.int32),
        pltpu.SMEM((1, 4), jnp.int32),
        pltpu.VMEM((1, 2, 576), BF),
        pltpu.VMEM((1, 2, 1792), BF),
        pltpu.VMEM((14, 128), F32),
        pltpu.SMEM((1, 1), jnp.int32),
        dma((13,)),
        dma((4,)),
        dma((4,)),
        dma((2, 8)),
        dma((2, 2, 4)),
        dma((4,)),
        dma((4,)),
        dma((8,)),
        dma((8,)),
        dma((2, 2, 2)),
        dma((2, 2, 2)),
        dma((2, 2, 8)),
        dma((2, 2, 8)),
        dma((2, 2, 8)),
        dma((2, 2, 8)),
        dma((2, 8)),
        dma((2, 8)),
        dma((2, 8)),
        dma((2, 8)),
        dma((2, 8)),
        dma((2, 8)),
        dma((2, 4)),
        dma((2, 4)),
        dma((2, 4)),
        dma((2, 4)),
    ]
    return pl.pallas_call(
        kernel,
        out_shape=jax.ShapeDtypeStruct((1, 2, 1792), BF),
        in_specs=[hbm] * 13,
        out_specs=vmem,
        scratch_shapes=scratch,
        compiler_params=pltpu.CompilerParams(
            collective_id=0, has_side_effects=True, vmem_limit_bytes=60 * 1024 * 1024
        ),
        cost_estimate=pl.CostEstimate(
            flops=2_000_000_000, bytes_accessed=6_000_000, transcendentals=250_000
        ),
    )(
        lengths.reshape(1, 1),
        table,
        slot_of,
        new_kv,
        resid,
        gain.reshape(14, 128),
        cache,
        sent,
        queries,
        w_ov,
        w_gate.T,
        w_up.T,
        w_down,
    )


def solution(mesh):
    in_specs = (
        P(("section", "dp"), "tp", None, None),
        P(("section", "dp"), "tp", None, None),
        P(("section", "dp"), "tp"),
        P(("section", "dp"), "tp"),
        P(("section", "dp")),
        P(("section", "dp"), None, None),
        P(("section", "dp"), None, None, None),
        P(("section", "dp"), None, "tp"),
        P("tp"),
        P(("section", "dp"), "tp"),
        P("tp", ("section", "dp")),
        P("tp", ("section", "dp")),
        P(("section", "dp"), "tp"),
    )
    out_specs = P(("section", "dp"), None, "tp")
    return jax.shard_map(body, mesh=mesh, in_specs=in_specs, out_specs=out_specs, check_vma=False)
```
